512 devices in a mesh: section: 8 (over z), row: 4 (over x_hi, core), col: 16 (over x_lo, y).
Axes of the slice: x: 4 (x_hi: 2, x_lo: 2; x = x_hi * 2 + x_lo), y: 8, z: 8, core: 2. Of those that a mesh axis runs over, the one named last changes fastest.
Arguments:
- hidden_in: bfloat16 [8, 512, 8192], P('section', 'col', 'row'), may hold values from -600 to 600
- norm_gain: float32 [8, 8192], P('section', 'row'), may hold values from 0.1 to 1.9
- q_weight: bfloat16 [8, 8192, 8192], P('section', 'row', 'col'), may hold values from -0.0625 to 0.0625
- kv_weight: bfloat16 [8, 8192, 2048], P('section', 'row', 'col'), may hold values from -0.0625 to 0.0625
- kv_cache: bfloat16 [8, 32, 1024, 2, 1024], P('section', 'col', 'row'), may hold values from -110 to 110
- lengths: int32 [8, 32], P('section', 'col'), may hold values from 768 to 1024, as said below
Outputs:
- handed: bfloat16 [8, 512, 8192], P('section', 'col', 'row')
- new_kv: bfloat16 [8, 512, 2048], P('section', 'col')
The draws below stay inside these ranges and needn't reach their ends.
Inputs may be any that keep to these rules, and one draw needn't show every extreme that they name: `lengths`: in every section some prompt uses exactly 1024 positions.
All inputs are finite; a program needn't handle non-finite values.
Results may differ from the reference program's by a relative error of at most 0.023.
Values may be sent and summed in bfloat16 or wider, within the bound.
No kernel may reach another device: no remote copies, remote signals or barrier semaphores. Data moves between devices by JAX's collectives and lax.ppermute only.
A program may use at most 64 MiB of HBM per device.

```python
import jax
import jax.numpy as jnp
from jax import lax

D = 8192
HEADS = 64
KV_HEADS = 8
HEAD_DIM = 128
SAMPLES = 16
PROMPTS = 32
ROWS = 512
CACHE = 1024
N_SECTION = 8


def draw_hidden_in(key, part):
    key_base, key_rows = jax.random.split(key)
    column = jnp.arange(D, dtype=jnp.float32) / (D - 1)
    row_scale = jnp.power(10.0, jax.random.uniform(key_rows, (N_SECTION, ROWS, 1), jnp.float32))
    base = jnp.clip(jax.random.normal(key_base, (N_SECTION, ROWS, D), jnp.float32), -6.0, 6.0)
    column_scale = jnp.power(10.0, column)
    return (base * row_scale * column_scale[None, None, :]).astype(jnp.bfloat16)


def draw_kv_cache(key, part):
    key_base = jax.random.fold_in(key, 0)
    shape_full = (N_SECTION, PROMPTS, CACHE, 2, KV_HEADS * HEAD_DIM)
    base = jnp.clip(jax.random.normal(key_base, shape_full, jnp.float32), -6.0, 6.0)
    return base.astype(jnp.bfloat16)


def draw_lengths(key, part):
    key_lengths, key_top = jax.random.split(key)
    drawn = jax.random.randint(key_lengths, (N_SECTION, PROMPTS), 3 * CACHE // 4, CACHE + 1)
    chosen = jax.random.randint(key_top, (N_SECTION, 1), 0, PROMPTS)
    places = jnp.arange(PROMPTS, dtype=jnp.int32)[None, :]
    return jnp.where(places == chosen, CACHE, drawn).astype(jnp.int32)


def block_scale(stream_key, shape, shards, least, high):
    level, own = 1.0, jax.random.fold_in(stream_key, 6)
    for position, parts in shards:
        heights = jnp.exp(jax.random.uniform(jax.random.fold_in(own, position), (parts,), jnp.float32, least / len(shards), high / len(shards)))
        level = level * jnp.repeat(heights, shape[position] // parts).reshape([-1 if axis == position else 1 for axis in range(len(shape))])
    return level


def normal_values(own_key, shape, scale, limit, pieces=(), kind=jnp.bfloat16):
    level = block_scale(own_key, shape, pieces, -0.22, 0.18) if pieces else 1.0
    array = jax.random.normal(own_key, shape, jnp.float32) * scale * level
    return jnp.minimum(jnp.maximum(array, -limit), limit).astype(kind)


def setup_inputs(seed: int = 0) -> dict:
    splits = jax.random.split(jax.random.key(seed), 7)
    hidden_in = draw_hidden_in(jax.random.fold_in(splits[6], 71), 0)
    norm_gain = jnp.clip(1.0 + 0.18 * jax.random.normal(splits[1], (N_SECTION, D), jnp.float32), 0.1, 1.9)
    q_weight = normal_values(splits[2], (N_SECTION, D, HEADS * HEAD_DIM), D ** -0.5, 0.0625, ((0, 8), (1, 4), (2, 16)))
    kv_weight = normal_values(splits[3], (N_SECTION, D, 2 * KV_HEADS * HEAD_DIM), D ** -0.5, 0.0625, ((0, 8), (1, 4), (2, 16)))
    kv_cache = draw_kv_cache(jax.random.fold_in(splits[6], 71), 0)
    lengths = draw_lengths(jax.random.fold_in(splits[6], 71), 0)
    return {"hidden_in": hidden_in, "norm_gain": norm_gain, "q_weight": q_weight, "kv_weight": kv_weight, "kv_cache": kv_cache, "lengths": lengths}


EPSILON = 1e-05
FLOOR = -1e+30

def attend(query_heads, cache_keys, cache_values, length, new_keys, new_values):
    score_scale = HEAD_DIM ** (-0.5)
    scores = jnp.einsum('sghd,tgd->sght', query_heads.astype(jnp.float32), cache_keys.astype(jnp.float32)) * score_scale
    own_score = jnp.einsum('sghd,sgd->sgh', query_heads.astype(jnp.float32), new_keys.astype(jnp.float32)) * score_scale
    in_range = jnp.arange(CACHE, dtype=jnp.int32) < length
    top_score = jnp.maximum(lax.optimization_barrier(jnp.max(jnp.where(in_range, scores, FLOOR), axis=-1)), own_score)
    weights = jnp.where(in_range, jnp.exp(scores - top_score[..., None]), 0.0)
    own_weight = jnp.exp(own_score - top_score)
    total_weight = lax.optimization_barrier(jnp.sum(weights, axis=-1)) + own_weight
    rounded = lax.optimization_barrier(weights.astype(jnp.bfloat16)).astype(jnp.float32)
    own_rounded = lax.optimization_barrier(own_weight.astype(jnp.bfloat16)).astype(jnp.float32)
    numerator = jnp.einsum('sght,tgd->sghd', rounded, cache_values.astype(jnp.float32))
    numerator = numerator + own_rounded[..., None] * new_values.astype(jnp.float32)[:, :, None, :]
    return (numerator / total_weight[..., None]).astype(jnp.bfloat16)

def layer_step(hidden, gain, query_weight, pair_weight, cache_block, prompt_lengths):
    widened = hidden.astype(jnp.float32)
    mean_square = lax.optimization_barrier(jnp.mean(widened * widened, axis=-1))
    normed = (widened * lax.rsqrt(mean_square + EPSILON)[:, None] * gain[None, :]).astype(jnp.bfloat16)
    query = jnp.dot(normed, query_weight, preferred_element_type=jnp.float32).astype(jnp.bfloat16)
    new_kv = jnp.dot(normed, pair_weight, preferred_element_type=jnp.float32).astype(jnp.bfloat16)
    prompt_count = prompt_lengths.shape[0]
    group_size = HEADS // KV_HEADS
    query_heads = query.reshape(prompt_count, SAMPLES, KV_HEADS, group_size, HEAD_DIM)
    new_keys = new_kv[:, :KV_HEADS * HEAD_DIM].reshape(prompt_count, SAMPLES, KV_HEADS, HEAD_DIM)
    new_values = new_kv[:, KV_HEADS * HEAD_DIM:].reshape(prompt_count, SAMPLES, KV_HEADS, HEAD_DIM)
    cache_keys = cache_block[:, :, 0].reshape(prompt_count, CACHE, KV_HEADS, HEAD_DIM)
    cache_values = cache_block[:, :, 1].reshape(prompt_count, CACHE, KV_HEADS, HEAD_DIM)
    attended = lax.map(lambda items: attend(*items), (query_heads, cache_keys, cache_values, prompt_lengths, new_keys, new_values))
    return (attended.reshape(prompt_count * SAMPLES, HEADS * HEAD_DIM), new_kv)

def reference(hidden_in, norm_gain, q_weight, kv_weight, kv_cache, lengths):
    attended, new_kv = lax.map(lambda items: layer_step(*items), (hidden_in, norm_gain, q_weight, kv_weight, kv_cache, lengths))
    handed = jnp.roll(attended, 1, axis=0)
    return (handed, new_kv)
```

```python
import jax
import jax.numpy as jnp
from jax import lax
from jax.experimental import pallas as pl
from jax.experimental.pallas import tpu as pltpu
from jax.sharding import Mesh
from jax.sharding import PartitionSpec as P

HEAD_DIM = 128
EPSILON = 1e-05
FLOOR = -1e30
ROW = ("xh", "co")
COL = ("xl", "y")
BF = jnp.bfloat16
F32 = jnp.float32


def attend_kernel(lengths_ref, parts_ref, scale_ref, cache_ref, out_ref, pair_ref):
    sources, blocks, rows, _ = parts_ref.shape
    _, prompts, _, heads, chunk, dim = cache_ref.shape
    samples = rows // prompts
    scale = scale_ref[...]
    total = []
    for j in range(blocks):
        part = parts_ref[0, j].astype(F32)
        for s in range(1, sources):
            part = part + parts_ref[s, j].astype(F32)
        total.append((part * scale).astype(BF))
    per_block = 512 // dim
    for j in range(blocks):
        pair_ref[j] = total[j][:, 512:]
    for p in range(prompts):
        length = lengths_ref[0, p]
        here = slice(p * samples, (p + 1) * samples)
        for g in range(heads):
            names = [(j, h) for j in (2 * g, 2 * g + 1) for h in range(per_block)]
            query = jnp.concatenate(
                [total[j][here, h * dim : (h + 1) * dim] for j, h in names], axis=0
            )
            new_key = total[g][here, 512:].astype(F32)
            new_value = total[2 + g][here, 512:].astype(F32)
            new_key = jnp.concatenate([new_key] * len(names), axis=0)
            new_value = jnp.concatenate([new_value] * len(names), axis=0)
            factor = dim**-0.5
            own = jnp.sum(query.astype(F32) * new_key, axis=1, keepdims=True) * factor
            scores = []
            top = own
            for s in range(sources):
                block = lax.dot_general(
                    query,
                    cache_ref[s, p, 0, g],
                    (((1,), (1,)), ((), ())),
                    preferred_element_type=F32,
                )
                place = s * chunk + lax.broadcasted_iota(jnp.int32, block.shape, 1)
                block = jnp.where(place < length, block * factor, FLOOR)
                top = jnp.maximum(top, jnp.max(block, axis=1, keepdims=True))
                scores.append(block)
            own_weight = jnp.exp(own - top)
            weight_sum = own_weight
            value = own_weight.astype(BF).astype(F32) * new_value
            for s in range(sources):
                weight = jnp.exp(scores[s] - top)
                weight_sum = weight_sum + jnp.sum(weight, axis=1, keepdims=True)
                value = value + jnp.dot(
                    weight.astype(BF), cache_ref[s, p, 1, g], preferred_element_type=F32
                )
            result = (value / weight_sum).astype(BF)
            for n, (j, h) in enumerate(names):
                at = (j * per_block + h) * dim
                out_ref[here, at : at + dim] = result[n * samples : (n + 1) * samples]


def attend(lengths, parts, scale, cache):
    rows = parts.shape[2]
    vmem = pl.BlockSpec(memory_space=pltpu.VMEM)
    return pl.pallas_call(
        attend_kernel,
        out_shape=(
            jax.ShapeDtypeStruct((rows, 2048), BF),
            jax.ShapeDtypeStruct((4, rows, HEAD_DIM), BF),
        ),
        in_specs=[pl.BlockSpec(memory_space=pltpu.SMEM), vmem, vmem, vmem],
        out_specs=(vmem, vmem),
        compiler_params=pltpu.CompilerParams(vmem_limit_bytes=32 * 1024 * 1024),
        name="attend",
    )(lengths, parts, scale, cache)


def shards(hidden_in, norm_gain, q_weight, kv_weight, kv_cache, lengths):
    rows = hidden_in.shape[1]
    width = hidden_in.shape[2]
    col_count = 16
    row_count = 4
    widened = hidden_in[0].astype(F32)
    sent = (widened * norm_gain[0][None, :]).astype(BF)
    gathered = lax.all_to_all(
        jnp.broadcast_to(sent[None], (col_count, rows, width)), COL, 0, 0
    )
    squares = lax.psum(jnp.sum(widened * widened, axis=1), ROW)
    scale = lax.rsqrt(squares / (width * row_count) + EPSILON)[:, None]
    prompts, chunk = kv_cache.shape[1], kv_cache.shape[2]
    cache = kv_cache[0].reshape(prompts, chunk, 2, row_count, 2, HEAD_DIM)
    cache = lax.all_to_all(cache.transpose(3, 0, 2, 4, 1, 5), ROW, 0, 0)
    flat = gathered.reshape(col_count * rows, width)
    query_part = jnp.dot(flat, q_weight[0], preferred_element_type=F32).astype(BF)
    pair_part = jnp.dot(flat, kv_weight[0], preferred_element_type=F32).astype(BF)
    both = jnp.concatenate([query_part, pair_part], axis=1).reshape(col_count, rows, -1)
    both = lax.all_to_all(both, COL, 0, 0)
    query_blocks = both[:, :, :512].reshape(row_count, 4, rows, 512)
    pair_blocks = both[:, :, 512:].reshape(2, row_count, 2, rows, HEAD_DIM)
    pair_blocks = pair_blocks.transpose(1, 0, 2, 3, 4).reshape(row_count, 4, rows, HEAD_DIM)
    parts = jnp.concatenate([query_blocks, pair_blocks], axis=3)
    parts = lax.all_to_all(parts, ROW, 0, 0)
    attended, pairs = attend(lengths, parts, scale, cache)
    count = 8
    handed = lax.ppermute(attended[None], "z", [((i - 1) % count, i) for i in range(count)])
    pairs = lax.all_gather(pairs, ROW)
    new_kv = pairs.reshape(row_count, 2, 2, rows, HEAD_DIM).transpose(3, 1, 0, 2, 4)
    return (handed, new_kv.reshape(1, rows, -1))


def solution(mesh):
    fine = Mesh(mesh.devices.reshape(8, 2, 2, 2, 8), ("z", "xh", "co", "xl", "y"))
    return jax.shard_map(
        shards,
        mesh=fine,
        in_specs=(
            P("z", COL, ROW),
            P("z", ROW),
            P("z", ROW, COL),
            P("z", ROW, COL),
            P("z", COL, ROW, None, None),
            P("z", COL),
        ),
        out_specs=(P("z", COL, ROW), P("z", COL, None)),
        check_vma=False,
    )
```

```python
import jax
import jax.numpy as jnp
from jax import lax
from jax.experimental import pallas as pl
from jax.experimental.pallas import tpu as pltpu
from jax.sharding import Mesh
from jax.sharding import PartitionSpec as P

HEAD_DIM = 128
EPSILON = 1e-05
FLOOR = -1e30
ROW = ("xh", "co")
COL = ("xl", "y")
BF = jnp.bfloat16
F32 = jnp.float32
VMEM = pl.BlockSpec(memory_space=pltpu.VMEM)
SMEM = pl.BlockSpec(memory_space=pltpu.SMEM)
PARAMS = pltpu.CompilerParams(vmem_limit_bytes=40 * 1024 * 1024)


def project_kernel(place_ref, ring_ref, direct_ref, query_ref, pair_ref, out_ref):
    count, rows, width = ring_ref.shape
    half = rows // 2
    mine = place_ref[0] * count
    other = (1 - place_ref[0]) * count
    own = ring_ref[...].reshape(count * rows, width)
    theirs = direct_ref[...].reshape(count * rows, width)

    def store(block, start, lanes):
        block = block.astype(BF).reshape(count, 2, half, block.shape[1])
        for h in range(2):
            out_ref[h, pl.ds(start, count), :, lanes] = block[:, h]

    for weight_ref, lanes in ((query_ref, slice(0, 512)), (pair_ref, slice(512, 640))):
        store(jnp.dot(theirs, weight_ref[...], preferred_element_type=F32), other, lanes)
        store(jnp.dot(own, weight_ref[...], preferred_element_type=F32), mine, lanes)


def project(place, ring, direct, query_weight, pair_weight):
    return pl.pallas_call(
        project_kernel,
        out_shape=jax.ShapeDtypeStruct((2, 16, 16, 640), BF),
        in_specs=[SMEM, VMEM, VMEM, VMEM, VMEM],
        out_specs=VMEM,
        compiler_params=PARAMS,
        name="project",
    )(place, ring, direct, query_weight, pair_weight)


def attend_kernel(lengths_ref, place_ref, parts_ref, scale_ref, *refs):
    caches, out_ref, pair_ref = refs[:4], refs[4], refs[5]
    _, prompts, blocks, samples, _ = parts_ref.shape
    _, _, heads, chunk, dim = caches[0].shape
    per_block = 512 // dim
    factor = dim**-0.5
    place = place_ref[0]
    for p in range(prompts):
        length = lengths_ref[0, p]
        here = slice(p * samples, (p + 1) * samples)
        scale = scale_ref[here]
        total = []
        for j in range(blocks):
            part = parts_ref[0, p, j].astype(F32) + parts_ref[1, p, j].astype(F32)
            total.append((part * scale).astype(BF))
            pair_ref[j, here] = total[j][:, 512:]
        for g in range(heads):
            names = [(j, h) for j in (2 * g, 2 * g + 1) for h in range(per_block)]
            query = jnp.concatenate([total[j][:, h * dim : (h + 1) * dim] for j, h in names], axis=0)
            new_key = jnp.concatenate([total[g][:, 512:].astype(F32)] * len(names), axis=0)
            new_value = jnp.concatenate([total[2 + g][:, 512:].astype(F32)] * len(names), axis=0)
            own = jnp.sum(query.astype(F32) * new_key, axis=1, keepdims=True) * factor
            scores = []
            top = own
            for k in range(len(caches)):
                block = lax.dot_general(
                    query, caches[k][p, 0, g], (((1,), (1,)), ((), ())), preferred_element_type=F32
                )
                first = lax.rem(place + len(caches) - k, len(caches)) * chunk
                position = first + lax.broadcasted_iota(jnp.int32, block.shape, 1)
                block = jnp.where(position < length, block * factor, FLOOR)
                top = jnp.maximum(top, jnp.max(block, axis=1, keepdims=True))
                scores.append(block)
            own_weight = jnp.exp(own - top)
            weight_sum = own_weight
            value = own_weight.astype(BF).astype(F32) * new_value
            for k in range(len(caches)):
                weight = jnp.exp(scores[k] - top)
                weight_sum = weight_sum + jnp.sum(weight, axis=1, keepdims=True)
                value = value + jnp.dot(
                    weight.astype(BF), caches[k][p, 1, g], preferred_element_type=F32
                )
            result = (value / weight_sum).astype(BF)
            for n, (j, h) in enumerate(names):
                at = (j * per_block + h) * dim
                out_ref[here, at : at + dim] = result[n * samples : (n + 1) * samples]


def attend(lengths, place, parts, scale, caches):
    rows = parts.shape[1] * parts.shape[3]
    return pl.pallas_call(
        attend_kernel,
        out_shape=(
            jax.ShapeDtypeStruct((rows, 2048), BF),
            jax.ShapeDtypeStruct((4, rows, HEAD_DIM), BF),
        ),
        in_specs=[SMEM, SMEM] + [VMEM] * 6,
        out_specs=(VMEM, VMEM),
        compiler_params=PARAMS,
        name="attend",
    )(lengths, place, parts, scale, *caches)


def shards(hidden_in, norm_gain, q_weight, kv_weight, kv_cache, lengths):
    rows, width = hidden_in.shape[1:]
    row_count = 4
    row_index = lax.axis_index(ROW)
    widened = hidden_in[0].astype(F32)
    sent = (widened * norm_gain[0][None, :]).astype(BF)
    local_squares = jnp.sum(widened * widened, axis=1)

    ring = lax.all_gather(sent, "y")
    theirs = lax.ppermute(sent, "xl", [(0, 1), (1, 0)])
    direct = lax.all_to_all(jnp.broadcast_to(theirs[None], (8, rows, width)), "y", 0, 0)

    prompts, chunk = kv_cache.shape[1], kv_cache.shape[2]
    cache = kv_cache[0].reshape(prompts, chunk, 2, row_count, 2, HEAD_DIM).transpose(3, 0, 2, 4, 1, 5)
    caches = []
    for k in range(row_count):
        piece = lax.dynamic_index_in_dim(cache, (row_index + k) % row_count, 0, keepdims=False)
        if k:
            piece = lax.ppermute(piece, ROW, [(i, (i + k) % row_count) for i in range(row_count)])
        caches.append(piece)
    ring, direct, caches = lax.optimization_barrier((ring, direct, caches))

    partial = project(lax.axis_index("xl")[None], ring, direct, q_weight[0], kv_weight[0])
    partial = lax.all_to_all(partial, "co", 0, 0)
    both = (partial[0].astype(F32) + partial[1].astype(F32)).astype(BF)
    both = lax.all_to_all(both, COL, 0, 0)
    samples = both.shape[1]
    query_blocks = both[:, :, :512].reshape(row_count, 4, samples, 512)
    pair_blocks = both[:, :, 512:].reshape(2, row_count, 2, samples, HEAD_DIM)
    pair_blocks = pair_blocks.transpose(1, 0, 2, 3, 4).reshape(row_count, 4, samples, HEAD_DIM)
    parts = jnp.concatenate([query_blocks, pair_blocks], axis=3)
    parts = lax.all_to_all(parts, ROW, 0, 0).reshape((2, 2) + parts.shape[1:])

    squares = lax.psum(local_squares, ROW)
    scale = lax.rsqrt(squares / (width * row_count) + EPSILON)[:, None]
    attended, pairs = attend(lengths, row_index[None], parts, scale, caches)
    count = 8
    handed = lax.ppermute(attended[None], "z", [((i - 1) % count, i) for i in range(count)])
    pairs = lax.all_gather(pairs, ROW)
    new_kv = pairs.reshape(row_count, 2, 2, rows, HEAD_DIM).transpose(3, 1, 0, 2, 4)
    return (handed, new_kv.reshape(1, rows, -1))


def solution(mesh):
    fine = Mesh(mesh.devices.reshape(8, 2, 2, 2, 8), ("z", "xh", "co", "xl", "y"))
    return jax.shard_map(
        shards,
        mesh=fine,
        in_specs=(
            P("z", COL, ROW),
            P("z", ROW),
            P("z", ROW, COL),
            P("z", ROW, COL),
            P("z", COL, ROW, None, None),
            P("z", COL),
        ),
        out_specs=(P("z", COL, ROW), P("z", COL, None)),
        check_vma=False,
    )
```

```python
import jax
import jax.numpy as jnp
from jax import lax
from jax.experimental import pallas as pl
from jax.experimental.pallas import tpu as pltpu
from jax.sharding import Mesh
from jax.sharding import PartitionSpec as P

HEAD_DIM = 128
EPSILON = 1e-05
FLOOR = -1e30
ROW = ("xh", "co")
COL = ("xl", "y")
BF = jnp.bfloat16
F32 = jnp.float32
FIRST = 1152
VMEM = pl.BlockSpec(memory_space=pltpu.VMEM)
HBM = pl.BlockSpec(memory_space=pltpu.HBM)
SMEM = pl.BlockSpec(memory_space=pltpu.SMEM)
PARAMS = pltpu.CompilerParams(vmem_limit_bytes=32 * 1024 * 1024)


def project_kernel(place_ref, own_ref, theirs_ref, rest_ref, query_ref, pair_ref, out_ref, query, pair, sems):
    count, rows, first = own_ref.shape
    remainder = rest_ref.shape[2] // 2
    half = rows // 2
    mine = place_ref[0] * count
    other = (1 - place_ref[0]) * count
    copies = []
    for lines in (pl.ds(0, first), pl.ds(first, remainder)):
        for source, target in ((query_ref, query), (pair_ref, pair)):
            n = len(copies)
            copies.append(pltpu.make_async_copy(source.at[lines], target.at[lines], sems.at[n]))
    for copy in copies:
        copy.start()

    def flat(block):
        return block.reshape(count * rows, block.shape[2])

    def times(block, lines):
        return [
            jnp.dot(block, weight[lines], preferred_element_type=F32) for weight in (query, pair)
        ]

    copies[0].wait()
    copies[1].wait()
    former = [times(flat(ref[...]), slice(0, first)) for ref in (own_ref, theirs_ref)]
    copies[2].wait()
    copies[3].wait()
    for n, start in enumerate((mine, other)):
        block = flat(rest_ref[:, :, n * remainder : (n + 1) * remainder])
        latter = times(block, slice(first, first + remainder))
        for part, more, lanes in zip(former[n], latter, (slice(0, 512), slice(512, 640))):
            part = (part + more).astype(BF).reshape(count, 2, half, part.shape[1])
            for h in range(2):
                out_ref[h, pl.ds(start, count), :, lanes] = part[:, h]


def project(place, own, theirs, rest, query_weight, pair_weight):
    return pl.pallas_call(
        project_kernel,
        out_shape=jax.ShapeDtypeStruct((2, 16, 16, 640), BF),
        in_specs=[SMEM, VMEM, VMEM, VMEM, HBM, HBM],
        out_specs=VMEM,
        scratch_shapes=[
            pltpu.VMEM(query_weight.shape, BF),
            pltpu.VMEM(pair_weight.shape, BF),
            pltpu.SemaphoreType.DMA((4,)),
        ],
        compiler_params=PARAMS,
        name="project",
    )(place, own, theirs, rest, query_weight, pair_weight)


def pick_kernel(cache_ref, *refs):
    pieces, sems = refs[:4], refs[4]
    place = lax.axis_index(ROW)
    copies = []
    for k in range(4):
        for p in range(2):
            for g in range(2):
                at = pl.multiple_of((place ^ k) * 256 + g * HEAD_DIM, HEAD_DIM)
                source = cache_ref.at[p, :, :, pl.ds(at, HEAD_DIM)]
                n = len(copies)
                copies.append(pltpu.make_async_copy(source, pieces[k].at[p, g], sems.at[n]))
    for copy in copies:
        copy.start()
    for copy in copies:
        copy.wait()


def pick(cache):
    prompts, chunk = cache.shape[:2]
    piece = jax.ShapeDtypeStruct((prompts, 2, chunk, 2, HEAD_DIM), BF)
    return pl.pallas_call(
        pick_kernel,
        out_shape=[piece] * 4,
        in_specs=[HBM],
        out_specs=[HBM] * 4,
        scratch_shapes=[pltpu.SemaphoreType.DMA((16,))],
        name="pick",
    )(cache)


def attend_kernel(lengths_ref, place_ref, parts_ref, scale_ref, *refs):
    caches, out_ref, pair_ref = refs[:4], refs[4], refs[5]
    _, prompts, blocks, samples, _ = parts_ref.shape
    _, heads, chunk, dim = caches[0].shape
    per_block = 512 // dim
    factor = dim**-0.5
    place = place_ref[0]
    column = lax.broadcasted_iota(jnp.int32, (1, chunk), 1)
    is_key = column % 2 == 0
    positions = []
    for k in range(len(caches)):
        first = (place ^ k) * (chunk // 2)
        positions.append(jnp.where(is_key, first + column // 2, 2**30))
    for p in range(prompts):
        length = lengths_ref[0, p]
        here = slice(p * samples, (p + 1) * samples)
        scale = scale_ref[here]
        total = []
        for j in range(blocks):
            part = parts_ref[0, p, j].astype(F32) + parts_ref[1, p, j].astype(F32)
            total.append((part * scale).astype(BF))
            pair_ref[j, here] = total[j][:, 512:]
        for g in range(heads):
            names = [(j, h) for j in (2 * g, 2 * g + 1) for h in range(per_block)]
            query = jnp.concatenate([total[j][:, h * dim : (h + 1) * dim] for j, h in names], axis=0)
            new_key = jnp.concatenate([total[g][:, 512:].astype(F32)] * len(names), axis=0)
            new_value = jnp.concatenate([total[2 + g][:, 512:].astype(F32)] * len(names), axis=0)
            own = jnp.sum(query.astype(F32) * new_key, axis=1, keepdims=True) * factor
            scores = []
            top = own
            for k in range(len(caches)):
                block = lax.dot_general(
                    query, caches[k][p, g], (((1,), (1,)), ((), ())), preferred_element_type=F32
                )
                block = jnp.where(positions[k] < length, block * factor, FLOOR)
                top = jnp.maximum(top, jnp.max(block, axis=1, keepdims=True))
                scores.append(block)
            own_weight = jnp.exp(own - top)
            weight_sum = own_weight
            value = own_weight.astype(BF).astype(F32) * new_value
            for k in range(len(caches)):
                weight = jnp.exp(scores[k] - top)
                weight_sum = weight_sum + jnp.sum(weight, axis=1, keepdims=True)
                weight = pltpu.roll(weight, 1, 1).astype(BF)
                value = value + jnp.dot(weight, caches[k][p, g], preferred_element_type=F32)
            result = (value / weight_sum).astype(BF)
            for n, (j, h) in enumerate(names):
                at = (j * per_block + h) * dim
                out_ref[here, at : at + dim] = result[n * samples : (n + 1) * samples]


def attend(lengths, place, parts, scale, caches):
    rows = parts.shape[1] * parts.shape[3]
    return pl.pallas_call(
        attend_kernel,
        out_shape=(
            jax.ShapeDtypeStruct((rows, 2048), BF),
            jax.ShapeDtypeStruct((4, rows, HEAD_DIM), BF),
        ),
        in_specs=[SMEM, SMEM] + [VMEM] * 6,
        out_specs=(VMEM, VMEM),
        compiler_params=PARAMS,
        name="attend",
    )(lengths, place, parts, scale, *caches)


def shards(hidden_in, norm_gain, q_weight, kv_weight, kv_cache, lengths):
    rows, width = hidden_in.shape[1:]
    row_count = 4
    row_index = lax.axis_index(ROW)
    widened = hidden_in[0].astype(F32)
    sent = (widened * norm_gain[0][None, :]).astype(BF)
    local_squares = jnp.sum(widened * widened, axis=1)
    swap = [(0, 1), (1, 0)]

    def spread(block):
        return lax.all_to_all(jnp.broadcast_to(block[None], (8,) + block.shape), "y", 0, 0)

    own = spread(sent[:, :FIRST])
    rest = sent[:, FIRST:]
    rest = jnp.concatenate([rest, lax.ppermute(rest, "xl", swap)], axis=1)
    own, rest, pieces = lax.optimization_barrier((own, rest, pick(kv_cache[0])))
    theirs = lax.ppermute(own, "xl", swap)
    rest = spread(rest)

    caches = []
    for k, piece in enumerate(pieces):
        if k:
            piece = lax.ppermute(piece, ROW, [(i, i ^ k) for i in range(row_count)])
        caches.append(piece.reshape(piece.shape[0], 2, -1, HEAD_DIM))

    place = lax.axis_index("xl")[None]
    partial = project(place, own, theirs, rest, q_weight[0], kv_weight[0])
    partial = lax.all_to_all(partial, "co", 0, 0)
    both = (partial[0].astype(F32) + partial[1].astype(F32)).astype(BF)
    both, local_squares, caches = lax.optimization_barrier((both, local_squares, caches))
    both = lax.all_to_all(both, COL, 0, 0)
    squares = lax.psum(local_squares, ROW)
    both, squares = lax.optimization_barrier((both, squares))
    samples = both.shape[1]
    query_blocks = both[:, :, :512].reshape(row_count, 4, samples, 512)
    pair_blocks = both[:, :, 512:].reshape(2, row_count, 2, samples, HEAD_DIM)
    pair_blocks = pair_blocks.transpose(1, 0, 2, 3, 4).reshape(row_count, 4, samples, HEAD_DIM)
    parts = jnp.concatenate([query_blocks, pair_blocks], axis=3)
    parts = lax.all_to_all(parts, ROW, 0, 0).reshape((2, 2) + parts.shape[1:])

    scale = lax.rsqrt(squares / (width * row_count) + EPSILON)[:, None]
    attended, pairs = attend(lengths, row_index[None], parts, scale, caches)
    count = 8
    handed = lax.ppermute(attended[None], "z", [((i - 1) % count, i) for i in range(count)])
    pairs = lax.all_gather(pairs, ROW)
    new_kv = pairs.reshape(row_count, 2, 2, rows, HEAD_DIM).transpose(3, 1, 0, 2, 4)
    return (handed, new_kv.reshape(1, rows, -1))


def solution(mesh):
    fine = Mesh(mesh.devices.reshape(8, 2, 2, 2, 8), ("z", "xh", "co", "xl", "y"))
    return jax.shard_map(
        shards,
        mesh=fine,
        in_specs=(
            P("z", COL, ROW),
            P("z", ROW),
            P("z", ROW, COL),
            P("z", ROW, COL),
            P("z", COL, ROW, None, None),
            P("z", COL),
        ),
        out_specs=(P("z", COL, ROW), P("z", COL, None)),
        check_vma=False,
    )
```

```python
import jax
import jax.numpy as jnp
from jax import lax
from jax.experimental import pallas as pl
from jax.experimental.pallas import tpu as pltpu
from jax.sharding import Mesh
from jax.sharding import PartitionSpec as P

HEAD_DIM = 128
EPSILON = 1e-05
FLOOR = -1e30
ROW = ("xh", "co")
COL = ("xl", "y")
BF = jnp.bfloat16
F32 = jnp.float32
FIRST = 1280
VMEM = pl.BlockSpec(memory_space=pltpu.VMEM)
HBM = pl.BlockSpec(memory_space=pltpu.HBM)
SMEM = pl.BlockSpec(memory_space=pltpu.SMEM)
PARAMS = pltpu.CompilerParams(vmem_limit_bytes=32 * 1024 * 1024)
FULL = pltpu.CompilerParams(vmem_limit_bytes=56 * 1024 * 1024)


def project_kernel(place_ref, own_ref, theirs_ref, rest_ref, query_ref, pair_ref, out_ref, query, pair, sems):
    count, rows, first = own_ref.shape
    remainder = rest_ref.shape[2] // 2
    half = rows // 2
    mine = place_ref[0] * count
    other = (1 - place_ref[0]) * count
    copies = []
    for lines in (pl.ds(0, first), pl.ds(first, remainder)):
        for source, target in ((query_ref, query), (pair_ref, pair)):
            n = len(copies)
            copies.append(pltpu.make_async_copy(source.at[lines], target.at[lines], sems.at[n]))
    for copy in copies:
        copy.start()

    def flat(block):
        return block.reshape(count * rows, block.shape[2])

    def times(block, lines):
        return [
            jnp.dot(block, weight[lines], preferred_element_type=F32) for weight in (query, pair)
        ]

    copies[0].wait()
    copies[1].wait()
    former = [times(flat(ref[...]), slice(0, first)) for ref in (own_ref, theirs_ref)]
    copies[2].wait()
    copies[3].wait()
    for n, start in enumerate((mine, other)):
        block = flat(rest_ref[:, :, n * remainder : (n + 1) * remainder])
        latter = times(block, slice(first, first + remainder))
        for part, more, lanes in zip(former[n], latter, (slice(0, 512), slice(512, 640))):
            part = (part + more).astype(BF).reshape(count, 2, half, part.shape[1])
            for h in range(2):
                out_ref[h, pl.ds(start, count), :, lanes] = part[:, h]


def project(place, own, theirs, rest, query_weight, pair_weight):
    return pl.pallas_call(
        project_kernel,
        out_shape=jax.ShapeDtypeStruct((2, 16, 16, 640), BF),
        in_specs=[SMEM, VMEM, VMEM, VMEM, HBM, HBM],
        out_specs=VMEM,
        scratch_shapes=[
            pltpu.VMEM(query_weight.shape, BF),
            pltpu.VMEM(pair_weight.shape, BF),
            pltpu.SemaphoreType.DMA((4,)),
        ],
        compiler_params=FULL,
        name="project",
    )(place, own, theirs, rest, query_weight, pair_weight)


def pick_kernel(place_ref, cache_ref, *pieces):
    for k, piece_ref in enumerate(pieces):
        for g in range(2):
            at = pl.multiple_of((place_ref[0] ^ k) * 256 + g * HEAD_DIM, HEAD_DIM)
            block = cache_ref[0, :, :, pl.ds(at, HEAD_DIM)]
            for v in range(2):
                piece_ref[0, v, g] = block[:, v, :]


def pick(place, cache):
    prompts, chunk = cache.shape[:2]
    return pl.pallas_call(
        pick_kernel,
        grid=(prompts,),
        out_shape=[jax.ShapeDtypeStruct((prompts, 2, 2, chunk, HEAD_DIM), BF)] * 4,
        in_specs=[SMEM, pl.BlockSpec((1,) + cache.shape[1:], lambda p: (p, 0, 0, 0))],
        out_specs=[pl.BlockSpec((1, 2, 2, chunk, HEAD_DIM), lambda p: (p, 0, 0, 0, 0))] * 4,
        compiler_params=PARAMS,
        name="pick",
    )(place, cache)


def arrange_kernel(both_ref, parts_ref):
    for j in range(4):
        for a in range(4):
            parts_ref[a, j, :, :512] = both_ref[4 * a + j, :, :512]
        pairs = [both_ref[4 * j + i, :, 512:] for i in range(4)]
        pairs = jnp.concatenate(pairs, axis=1)
        for a in range(4):
            parts_ref[a, j, :, 512:] = pairs


def arrange(both):
    return pl.pallas_call(
        arrange_kernel,
        out_shape=jax.ShapeDtypeStruct((4, 4, both.shape[1], 1024), BF),
        in_specs=[VMEM],
        out_specs=VMEM,
        compiler_params=PARAMS,
        name="arrange",
    )(both)


def attend_kernel(lengths_ref, place_ref, parts_ref, scale_ref, *refs):
    caches, out_ref, pair_ref = refs[:4], refs[4], refs[5]
    _, prompts, blocks, samples, _ = parts_ref.shape
    _, _, heads, chunk, dim = caches[0].shape
    per_block = 512 // dim
    factor = dim**-0.5
    place = place_ref[0]
    column = lax.broadcasted_iota(jnp.int32, (1, chunk), 1)
    positions = [(place ^ k) * chunk + column for k in range(len(caches))]
    for p in range(prompts):
        length = lengths_ref[0, p]
        here = slice(p * samples, (p + 1) * samples)
        scale = scale_ref[here]

        def total(block, lanes):
            part = parts_ref[0, p, block, :, lanes].astype(F32)
            part = part + parts_ref[1, p, block, :, lanes].astype(F32)
            return (part * scale).astype(BF)

        for j in range(blocks):
            pair_ref[here, j * 512 : (j + 1) * 512] = total(j, slice(512, 1024))
        for g in range(heads):
            head = place * heads + g
            lanes = pl.ds(pl.multiple_of(512 + lax.rem(head, 4) * dim, dim), dim)
            new_key = total(head // 4, lanes).astype(F32)
            new_value = total(2 + head // 4, lanes).astype(F32)
            names = [(j, h) for j in (2 * g, 2 * g + 1) for h in range(per_block)]
            queries = [total(j, slice(0, 512)) for j in (2 * g, 2 * g + 1)]
            query = [q[:, h * dim : (h + 1) * dim] for q in queries for h in range(per_block)]
            query = jnp.concatenate(query, axis=0)
            new_key = jnp.concatenate([new_key] * len(names), axis=0)
            new_value = jnp.concatenate([new_value] * len(names), axis=0)
            own = jnp.sum(query.astype(F32) * new_key, axis=1, keepdims=True) * factor
            scores = []
            top = own
            for k in range(len(caches)):
                block = lax.dot_general(
                    query, caches[k][p, 0, g], (((1,), (1,)), ((), ())), preferred_element_type=F32
                )
                block = jnp.where(positions[k] < length, block * factor, FLOOR)
                top = jnp.maximum(top, jnp.max(block, axis=1, keepdims=True))
                scores.append(block)
            own_weight = jnp.exp(own - top)
            weight_sum = own_weight
            value = own_weight.astype(BF).astype(F32) * new_value
            for k in range(len(caches)):
                weight = jnp.exp(scores[k] - top)
                weight_sum = weight_sum + jnp.sum(weight, axis=1, keepdims=True)
                value = value + jnp.dot(
                    weight.astype(BF), caches[k][p, 1, g], preferred_element_type=F32
                )
            result = (value / weight_sum).astype(BF)
            for n, (j, h) in enumerate(names):
                at = (j * per_block + h) * dim
                out_ref[here, at : at + dim] = result[n * samples : (n + 1) * samples]


def attend(lengths, place, parts, scale, caches):
    rows = parts.shape[1] * parts.shape[3]
    return pl.pallas_call(
        attend_kernel,
        out_shape=[jax.ShapeDtypeStruct((rows, 2048), BF)] * 2,
        in_specs=[SMEM, SMEM] + [VMEM] * 6,
        out_specs=(VMEM, VMEM),
        compiler_params=PARAMS,
        name="attend",
    )(lengths, place, parts, scale, *caches)


def shards(hidden_in, norm_gain, q_weight, kv_weight, kv_cache, lengths):
    rows, width = hidden_in.shape[1:]
    row_count = 4
    row_index = lax.axis_index(ROW)
    widened = hidden_in[0].astype(F32)
    sent = (widened * norm_gain[0][None, :]).astype(BF)
    local_squares = jnp.sum(widened * widened, axis=1)
    swap = [(0, 1), (1, 0)]

    def spread(block):
        return lax.all_to_all(jnp.broadcast_to(block[None], (8,) + block.shape), "y", 0, 0)

    own = spread(sent[:, :FIRST])
    rest = sent[:, FIRST:]
    rest = jnp.concatenate([rest, lax.ppermute(rest, "xl", swap)], axis=1)
    squares = lax.psum(local_squares, ROW)
    own, rest, pieces, squares = lax.optimization_barrier(
        (own, rest, pick(row_index[None], kv_cache[0]), squares)
    )
    theirs = lax.ppermute(own, "xl", swap)
    rest = spread(rest)

    caches = []
    for k, piece in enumerate(pieces):
        if k:
            piece = lax.ppermute(piece, ROW, [(i, i ^ k) for i in range(row_count)])
        caches.append(piece)

    place = lax.axis_index("xl")[None]
    partial = project(place, own, theirs, rest, q_weight[0], kv_weight[0])
    partial = lax.all_to_all(partial, "co", 0, 0)
    both = (partial[0].astype(F32) + partial[1].astype(F32)).astype(BF)
    both, caches = lax.optimization_barrier((both, caches))
    both = lax.all_to_all(both, COL, 0, 0)
    parts = lax.all_to_all(arrange(both), ROW, 0, 0)
    parts = parts.reshape((2, 2) + parts.shape[1:])

    scale = lax.rsqrt(squares / (width * row_count) + EPSILON)[:, None]
    attended, new_kv = attend(lengths, row_index[None], parts, scale, caches)
    count = 8
    handed = lax.ppermute(attended[None], "z", [((i - 1) % count, i) for i in range(count)])
    return (handed, new_kv[None])


def solution(mesh):
    fine = Mesh(mesh.devices.reshape(8, 2, 2, 2, 8), ("z", "xh", "co", "xl", "y"))
    return jax.shard_map(
        shards,
        mesh=fine,
        in_specs=(
            P("z", COL, ROW),
            P("z", ROW),
            P("z", ROW, COL),
            P("z", ROW, COL),
            P("z", COL, ROW, None, None),
            P("z", COL),
        ),
        out_specs=(P("z", COL, ROW), P("z", COL, None)),
        check_vma=False,
    )
```

```python
import jax
import jax.numpy as jnp
from jax import lax
from jax.experimental import pallas as pl
from jax.experimental.pallas import tpu as pltpu
from jax.sharding import Mesh
from jax.sharding import PartitionSpec as P

HEAD_DIM = 128
EPSILON = 1e-05
FLOOR = -1e30
ROW = ("xh", "co")
COL = ("xl", "y")
BF = jnp.bfloat16
F32 = jnp.float32
FIRST = 1152
VMEM = pl.BlockSpec(memory_space=pltpu.VMEM)
HBM = pl.BlockSpec(memory_space=pltpu.HBM)
SMEM = pl.BlockSpec(memory_space=pltpu.SMEM)
PARAMS = pltpu.CompilerParams(vmem_limit_bytes=32 * 1024 * 1024)
FULL = pltpu.CompilerParams(vmem_limit_bytes=56 * 1024 * 1024)


def project_kernel(place_ref, own_ref, theirs_ref, rest_ref, query_ref, pair_ref, out_ref, *scratch):
    own, theirs, rest, query, pair, sems = scratch
    count, rows, first = own_ref.shape
    remainder = rest_ref.shape[2] // 2
    half = rows // 2
    mine = place_ref[0] * count
    other = (1 - place_ref[0]) * count
    former_lines, latter_lines = pl.ds(0, first), pl.ds(first, remainder)
    moves = (
        (own_ref, own),
        (query_ref.at[former_lines], query.at[former_lines]),
        (pair_ref.at[former_lines], pair.at[former_lines]),
        (theirs_ref, theirs),
        (rest_ref, rest),
        (query_ref.at[latter_lines], query.at[latter_lines]),
        (pair_ref.at[latter_lines], pair.at[latter_lines]),
    )
    copies = [pltpu.make_async_copy(a, b, sems.at[n]) for n, (a, b) in enumerate(moves)]
    for copy in copies:
        copy.start()

    def times(block, lines):
        block = block.reshape(count * rows, block.shape[2])
        return [
            jnp.dot(block, weight[lines], preferred_element_type=F32) for weight in (query, pair)
        ]

    for copy in copies[:3]:
        copy.wait()
    former = [times(own[...], slice(0, first))]
    copies[3].wait()
    former.append(times(theirs[...], slice(0, first)))
    for copy in copies[4:]:
        copy.wait()
    for n, start in enumerate((mine, other)):
        block = rest[:, :, n * remainder : (n + 1) * remainder]
        latter = times(block, slice(first, first + remainder))
        for part, more, lanes in zip(former[n], latter, (slice(0, 512), slice(512, 640))):
            part = (part + more).astype(BF).reshape(count, 2, half, part.shape[1])
            for h in range(2):
                out_ref[h, pl.ds(start, count), :, lanes] = part[:, h]


def project(place, *operands):
    return pl.pallas_call(
        project_kernel,
        out_shape=jax.ShapeDtypeStruct((2, 16, 16, 640), BF),
        in_specs=[SMEM] + [HBM] * 5,
        out_specs=VMEM,
        scratch_shapes=[pltpu.VMEM(x.shape, BF) for x in operands] + [pltpu.SemaphoreType.DMA((7,))],
        compiler_params=FULL,
        name="project",
    )(place, *operands)


def pick(places, place, cache):
    prompts, chunk = cache.shape[:2]

    def pick_kernel(place_ref, cache_ref, *pieces):
        for k, piece_ref in zip(places, pieces):
            for g in range(2):
                at = pl.multiple_of((place_ref[0] ^ k) * 256 + g * HEAD_DIM, HEAD_DIM)
                block = cache_ref[0, :, :, pl.ds(at, HEAD_DIM)]
                for v in range(2):
                    piece_ref[0, v, g] = block[:, v, :]

    block = pl.BlockSpec((1, 2, 2, chunk, HEAD_DIM), lambda p: (p, 0, 0, 0, 0))
    return pl.pallas_call(
        pick_kernel,
        grid=(prompts,),
        out_shape=[jax.ShapeDtypeStruct((prompts, 2, 2, chunk, HEAD_DIM), BF)] * len(places),
        in_specs=[SMEM, pl.BlockSpec((1,) + cache.shape[1:], lambda p: (p, 0, 0, 0))],
        out_specs=[block] * len(places),
        compiler_params=PARAMS,
        name="pick",
    )(place, cache)


def arrange_kernel(both_ref, parts_ref):
    for j in range(4):
        for a in range(4):
            parts_ref[a, j, :, :512] = both_ref[4 * a + j, :, :512]
        pairs = [both_ref[4 * j + i, :, 512:] for i in range(4)]
        pairs = jnp.concatenate(pairs, axis=1)
        for a in range(4):
            parts_ref[a, j, :, 512:] = pairs


def arrange(both):
    return pl.pallas_call(
        arrange_kernel,
        out_shape=jax.ShapeDtypeStruct((4, 4, both.shape[1], 1024), BF),
        in_specs=[VMEM],
        out_specs=VMEM,
        compiler_params=PARAMS,
        name="arrange",
    )(both)


def attend_kernel(lengths_ref, place_ref, parts_ref, scale_ref, *refs):
    caches, out_ref, pair_ref = refs[:4], refs[4], refs[5]
    _, prompts, blocks, samples, _ = parts_ref.shape
    _, _, heads, chunk, dim = caches[0].shape
    per_block = 512 // dim
    factor = dim**-0.5
    place = place_ref[0]
    column = lax.broadcasted_iota(jnp.int32, (1, chunk), 1)
    positions = [(place ^ k) * chunk + column for k in range(len(caches))]
    for p in range(prompts):
        length = lengths_ref[0, p]
        here = slice(p * samples, (p + 1) * samples)
        scale = scale_ref[here]

        def total(block, lanes):
            part = parts_ref[0, p, block, :, lanes].astype(F32)
            part = part + parts_ref[1, p, block, :, lanes].astype(F32)
            return (part * scale).astype(BF)

        for j in range(blocks):
            pair_ref[here, j * 512 : (j + 1) * 512] = total(j, slice(512, 1024))
        for g in range(heads):
            head = place * heads + g
            lanes = pl.ds(pl.multiple_of(512 + lax.rem(head, 4) * dim, dim), dim)
            new_key = total(head // 4, lanes).astype(F32)
            new_value = total(2 + head // 4, lanes).astype(F32)
            names = [(j, h) for j in (2 * g, 2 * g + 1) for h in range(per_block)]
            queries = [total(j, slice(0, 512)) for j in (2 * g, 2 * g + 1)]
            query = [q[:, h * dim : (h + 1) * dim] for q in queries for h in range(per_block)]
            query = jnp.concatenate(query, axis=0)
            new_key = jnp.concatenate([new_key] * len(names), axis=0)
            new_value = jnp.concatenate([new_value] * len(names), axis=0)
            own = jnp.sum(query.astype(F32) * new_key, axis=1, keepdims=True) * factor
            scores = []
            top = own
            for k in range(len(caches)):
                block = lax.dot_general(
                    query, caches[k][p, 0, g], (((1,), (1,)), ((), ())), preferred_element_type=F32
                )
                block = jnp.where(positions[k] < length, block * factor, FLOOR)
                top = jnp.maximum(top, jnp.max(block, axis=1, keepdims=True))
                scores.append(block)
            own_weight = jnp.exp(own - top)
            weight_sum = own_weight
            value = own_weight.astype(BF).astype(F32) * new_value
            for k in range(len(caches)):
                weight = jnp.exp(scores[k] - top)
                weight_sum = weight_sum + jnp.sum(weight, axis=1, keepdims=True)
                value = value + jnp.dot(
                    weight.astype(BF), caches[k][p, 1, g], preferred_element_type=F32
                )
            result = (value / weight_sum).astype(BF)
            for n, (j, h) in enumerate(names):
                at = (j * per_block + h) * dim
                out_ref[here, at : at + dim] = result[n * samples : (n + 1) * samples]


def attend(lengths, place, parts, scale, caches):
    rows = parts.shape[1] * parts.shape[3]
    return pl.pallas_call(
        attend_kernel,
        out_shape=[jax.ShapeDtypeStruct((rows, 2048), BF)] * 2,
        in_specs=[SMEM, SMEM] + [VMEM] * 6,
        out_specs=(VMEM, VMEM),
        compiler_params=PARAMS,
        name="attend",
    )(lengths, place, parts, scale, *caches)


def shards(hidden_in, norm_gain, q_weight, kv_weight, kv_cache, lengths):
    rows, width = hidden_in.shape[1:]
    row_count = 4
    row_index = lax.axis_index(ROW)
    widened = hidden_in[0].astype(F32)
    sent = (widened * norm_gain[0][None, :]).astype(BF)
    local_squares = jnp.sum(widened * widened, axis=1)
    swap = [(0, 1), (1, 0)]

    def spread(block):
        return lax.all_to_all(jnp.broadcast_to(block[None], (8,) + block.shape), "y", 0, 0)

    def exchanged(piece, k):
        return lax.ppermute(piece, ROW, [(i, i ^ k) for i in range(row_count)])

    own = spread(sent[:, :FIRST])
    across = exchanged(pick((2,), row_index[None], kv_cache[0])[0], 2)
    rest = sent[:, FIRST:]
    rest = jnp.concatenate([rest, lax.ppermute(rest, "xl", swap)], axis=1)
    pieces = pick((0, 1, 3), row_index[None], kv_cache[0])
    own, rest, pieces, across, local_squares = lax.optimization_barrier(
        (own, rest, pieces, across, local_squares)
    )
    theirs = lax.ppermute(own, "xl", swap)
    rest = spread(rest)
    caches = [pieces[0], exchanged(pieces[1], 1), across, exchanged(pieces[2], 3)]
    squares = lax.psum(local_squares, ROW)
    theirs, rest, squares = lax.optimization_barrier((theirs, rest, squares))

    place = lax.axis_index("xl")[None]
    partial = project(place, own, theirs, rest, q_weight[0], kv_weight[0])
    partial = lax.all_to_all(partial, "co", 0, 0)
    both = (partial[0].astype(F32) + partial[1].astype(F32)).astype(BF)
    both, caches = lax.optimization_barrier((both, caches))
    both = lax.all_to_all(both, COL, 0, 0)
    parts = lax.all_to_all(arrange(both), ROW, 0, 0)
    parts = parts.reshape((2, 2) + parts.shape[1:])

    scale = lax.rsqrt(squares / (width * row_count) + EPSILON)[:, None]
    attended, new_kv = attend(lengths, row_index[None], parts, scale, caches)
    count = 8
    handed = lax.ppermute(attended[None], "z", [((i - 1) % count, i) for i in range(count)])
    return (handed, new_kv[None])


def solution(mesh):
    fine = Mesh(mesh.devices.reshape(8, 2, 2, 2, 8), ("z", "xh", "co", "xl", "y"))
    return jax.shard_map(
        shards,
        mesh=fine,
        in_specs=(
            P("z", COL, ROW),
            P("z", ROW),
            P("z", ROW, COL),
            P("z", ROW, COL),
            P("z", COL, ROW, None, None),
            P("z", COL),
        ),
        out_specs=(P("z", COL, ROW), P("z", COL, None)),
        check_vma=False,
    )
```

```python
import jax
import jax.numpy as jnp
from jax import lax
from jax.experimental import pallas as pl
from jax.experimental.pallas import tpu as pltpu
from jax.sharding import Mesh
from jax.sharding import PartitionSpec as P

HEAD_DIM = 128
EPSILON = 1e-05
FLOOR = -1e30
ROW = ("xh", "co")
COL = ("xl", "y")
BF = jnp.bfloat16
F32 = jnp.float32
FIRST = 1024
VMEM = pl.BlockSpec(memory_space=pltpu.VMEM)
HBM = pl.BlockSpec(memory_space=pltpu.HBM)
SMEM = pl.BlockSpec(memory_space=pltpu.SMEM)
PARAMS = pltpu.CompilerParams(vmem_limit_bytes=32 * 1024 * 1024)
FULL = pltpu.CompilerParams(vmem_limit_bytes=56 * 1024 * 1024)


def project_kernel(place_ref, own_ref, theirs_ref, rest_ref, query_ref, pair_ref, keep_ref, send_ref, *scratch):
    own, theirs, rest, query, pair, sems = scratch
    count, rows, first = own_ref.shape
    remainder = rest_ref.shape[2] // 2
    half = rows // 2
    mine = place_ref[0] * count
    other = (1 - place_ref[0]) * count
    former_lines, latter_lines = pl.ds(0, first), pl.ds(first, remainder)
    moves = (
        (own_ref, own),
        (query_ref.at[former_lines], query.at[former_lines]),
        (pair_ref.at[former_lines], pair.at[former_lines]),
        (theirs_ref, theirs),
        (rest_ref, rest),
        (query_ref.at[latter_lines], query.at[latter_lines]),
        (pair_ref.at[latter_lines], pair.at[latter_lines]),
    )
    copies = [pltpu.make_async_copy(a, b, sems.at[n]) for n, (a, b) in enumerate(moves)]
    for copy in copies:
        copy.start()

    def times(block, lines):
        block = block.reshape(count * rows, block.shape[2])
        return [
            jnp.dot(block, weight[lines], preferred_element_type=F32) for weight in (query, pair)
        ]

    for copy in copies[:3]:
        copy.wait()
    former = [times(own[...], slice(0, first))]
    copies[3].wait()
    former.append(times(theirs[...], slice(0, first)))
    for copy in copies[4:]:
        copy.wait()
    for n, start in enumerate((mine, other)):
        block = rest[:, :, n * remainder : (n + 1) * remainder]
        latter = times(block, slice(first, first + remainder))
        for part, more, lanes in zip(former[n], latter, (slice(0, 512), slice(512, 640))):
            part = (part + more).astype(BF).reshape(count, 2, half, part.shape[1])
            for core in range(2):

                @pl.when(place_ref[1] == core)
                def _():
                    keep_ref[pl.ds(start, count), :, lanes] = part[:, core]
                    send_ref[pl.ds(start, count), :, lanes] = part[:, 1 - core]


def project(place, *operands):
    return pl.pallas_call(
        project_kernel,
        out_shape=[jax.ShapeDtypeStruct((16, 16, 640), BF)] * 2,
        in_specs=[SMEM] + [HBM] * 5,
        out_specs=[VMEM] * 2,
        scratch_shapes=[pltpu.VMEM(x.shape, BF) for x in operands] + [pltpu.SemaphoreType.DMA((7,))],
        compiler_params=FULL,
        name="project",
    )(place, *operands)


def pick(places, place, cache):
    prompts, chunk = cache.shape[:2]

    def pick_kernel(place_ref, cache_ref, *pieces):
        for k, piece_ref in zip(places, pieces):
            for g in range(2):
                at = pl.multiple_of((place_ref[0] ^ k) * 256 + g * HEAD_DIM, HEAD_DIM)
                block = cache_ref[0, :, :, pl.ds(at, HEAD_DIM)]
                for v in range(2):
                    piece_ref[0, v, g] = block[:, v, :]

    block = pl.BlockSpec((1, 2, 2, chunk, HEAD_DIM), lambda p: (p, 0, 0, 0, 0))
    return pl.pallas_call(
        pick_kernel,
        grid=(prompts,),
        out_shape=[jax.ShapeDtypeStruct((prompts, 2, 2, chunk, HEAD_DIM), BF)] * len(places),
        in_specs=[SMEM, pl.BlockSpec((1,) + cache.shape[1:], lambda p: (p, 0, 0, 0))],
        out_specs=[block] * len(places),
        compiler_params=PARAMS,
        name="pick",
    )(place, cache)


def arrange_kernel(both_ref, parts_ref):
    for j in range(4):
        for a in range(4):
            parts_ref[a, j, :, :512] = both_ref[4 * a + j, :, :512]
        pairs = [both_ref[4 * j + i, :, 512:] for i in range(4)]
        pairs = jnp.concatenate(pairs, axis=1)
        for a in range(4):
            parts_ref[a, j, :, 512:] = pairs


def arrange(both):
    return pl.pallas_call(
        arrange_kernel,
        out_shape=jax.ShapeDtypeStruct((4, 4, both.shape[1], 1024), BF),
        in_specs=[VMEM],
        out_specs=VMEM,
        compiler_params=PARAMS,
        name="arrange",
    )(both)


def attend_kernel(lengths_ref, place_ref, parts_ref, scale_ref, *refs):
    caches, out_ref, pair_ref = refs[:4], refs[4], refs[5]
    _, prompts, blocks, samples, _ = parts_ref.shape
    _, _, heads, chunk, dim = caches[0].shape
    per_block = 512 // dim
    factor = dim**-0.5
    place = place_ref[0]
    column = lax.broadcasted_iota(jnp.int32, (1, chunk), 1)
    positions = [(place ^ k) * chunk + column for k in range(len(caches))]
    for p in range(prompts):
        length = lengths_ref[0, p]
        here = slice(p * samples, (p + 1) * samples)
        scale = scale_ref[here]

        def total(block, lanes):
            part = parts_ref[0, p, block, :, lanes].astype(F32)
            part = part + parts_ref[1, p, block, :, lanes].astype(F32)
            return (part * scale).astype(BF)

        for j in range(blocks):
            pair_ref[here, j * 512 : (j + 1) * 512] = total(j, slice(512, 1024))
        for g in range(heads):
            head = place * heads + g
            lanes = pl.ds(pl.multiple_of(512 + lax.rem(head, 4) * dim, dim), dim)
            new_key = total(head // 4, lanes).astype(F32)
            new_value = total(2 + head // 4, lanes).astype(F32)
            names = [(j, h) for j in (2 * g, 2 * g + 1) for h in range(per_block)]
            queries = [total(j, slice(0, 512)) for j in (2 * g, 2 * g + 1)]
            query = [q[:, h * dim : (h + 1) * dim] for q in queries for h in range(per_block)]
            query = jnp.concatenate(query, axis=0)
            new_key = jnp.concatenate([new_key] * len(names), axis=0)
            new_value = jnp.concatenate([new_value] * len(names), axis=0)
            own = jnp.sum(query.astype(F32) * new_key, axis=1, keepdims=True) * factor
            scores = []
            top = own
            for k in range(len(caches)):
                block = lax.dot_general(
                    query, caches[k][p, 0, g], (((1,), (1,)), ((), ())), preferred_element_type=F32
                )
                block = jnp.where(positions[k] < length, block * factor, FLOOR)
                top = jnp.maximum(top, jnp.max(block, axis=1, keepdims=True))
                scores.append(block)
            own_weight = jnp.exp(own - top)
            weight_sum = own_weight
            value = own_weight.astype(BF).astype(F32) * new_value
            for k in range(len(caches)):
                weight = jnp.exp(scores[k] - top)
                weight_sum = weight_sum + jnp.sum(weight, axis=1, keepdims=True)
                value = value + jnp.dot(
                    weight.astype(BF), caches[k][p, 1, g], preferred_element_type=F32
                )
            result = (value / weight_sum).astype(BF)
            for n, (j, h) in enumerate(names):
                at = (j * per_block + h) * dim
                out_ref[here, at : at + dim] = result[n * samples : (n + 1) * samples]


def attend(lengths, place, parts, scale, caches):
    rows = parts.shape[1] * parts.shape[3]
    return pl.pallas_call(
        attend_kernel,
        out_shape=[jax.ShapeDtypeStruct((rows, 2048), BF)] * 2,
        in_specs=[SMEM, SMEM] + [VMEM] * 6,
        out_specs=(VMEM, VMEM),
        compiler_params=PARAMS,
        name="attend",
    )(lengths, place, parts, scale, *caches)


def shards(hidden_in, norm_gain, q_weight, kv_weight, kv_cache, lengths):
    rows, width = hidden_in.shape[1:]
    row_count = 4
    row_index = lax.axis_index(ROW)
    widened = hidden_in[0].astype(F32)
    sent = (widened * norm_gain[0][None, :]).astype(BF)
    local_squares = jnp.sum(widened * widened, axis=1)
    swap = [(0, 1), (1, 0)]

    def spread(block):
        return lax.all_to_all(jnp.broadcast_to(block[None], (8,) + block.shape), "y", 0, 0)

    def exchanged(piece, k):
        return lax.ppermute(piece, ROW, [(i, i ^ k) for i in range(row_count)])

    own = spread(sent[:, :FIRST])
    across = exchanged(pick((2,), row_index[None], kv_cache[0])[0], 2)
    rest = sent[:, FIRST:]
    rest = jnp.concatenate([rest, lax.ppermute(rest, "xl", swap)], axis=1)
    pieces = pick((0, 1, 3), row_index[None], kv_cache[0])
    rest, own, pieces, across = lax.optimization_barrier((rest, own, pieces, across))
    theirs = lax.ppermute(own, "xl", swap)
    rest = spread(rest)
    caches = [pieces[0], exchanged(pieces[1], 1), across, exchanged(pieces[2], 3)]

    place = jnp.stack([lax.axis_index("xl"), lax.axis_index("co")])
    keep, send = project(place, own, theirs, rest, q_weight[0], kv_weight[0])
    send, caches = lax.optimization_barrier((send, caches))
    both = (keep.astype(F32) + lax.ppermute(send, "co", swap).astype(F32)).astype(BF)
    both, local_squares = lax.optimization_barrier((both, local_squares))
    both = lax.all_to_all(both, COL, 0, 0)
    squares = lax.psum(local_squares, ROW)
    both, squares = lax.optimization_barrier((both, squares))
    parts = lax.all_to_all(arrange(both), ROW, 0, 0)
    parts = parts.reshape((2, 2) + parts.shape[1:])

    scale = lax.rsqrt(squares / (width * row_count) + EPSILON)[:, None]
    attended, new_kv = attend(lengths, row_index[None], parts, scale, caches)
    count = 8
    handed = lax.ppermute(attended[None], "z", [((i - 1) % count, i) for i in range(count)])
    return (handed, new_kv[None])


def solution(mesh):
    fine = Mesh(mesh.devices.reshape(8, 2, 2, 2, 8), ("z", "xh", "co", "xl", "y"))
    return jax.shard_map(
        shards,
        mesh=fine,
        in_specs=(
            P("z", COL, ROW),
            P("z", ROW),
            P("z", ROW, COL),
            P("z", ROW, COL),
            P("z", COL, ROW, None, None),
            P("z", COL),
        ),
        out_specs=(P("z", COL, ROW), P("z", COL, None)),
        check_vma=False,
    )
```

```python
import jax
import jax.numpy as jnp
from jax import lax
from jax.experimental import pallas as pl
from jax.experimental.pallas import tpu as pltpu
from jax.sharding import Mesh
from jax.sharding import PartitionSpec as P

HEAD_DIM = 128
EPSILON = 1e-05
FLOOR = -1e30
ROW = ("xh", "co")
COL = ("xl", "y")
BF = jnp.bfloat16
F32 = jnp.float32
VMEM = pl.BlockSpec(memory_space=pltpu.VMEM)
HBM = pl.BlockSpec(memory_space=pltpu.HBM)
SMEM = pl.BlockSpec(memory_space=pltpu.SMEM)
PARAMS = pltpu.CompilerParams(vmem_limit_bytes=32 * 1024 * 1024)
FULL = pltpu.CompilerParams(vmem_limit_bytes=56 * 1024 * 1024)


def project_kernel(place_ref, gathered_ref, query_ref, pair_ref, keep_ref, send_ref, *scratch):
    gathered, query, pair, sems = scratch
    count, rows, width = gathered_ref.shape
    half = rows // 2
    step = count // 4
    moves = [(query_ref, query), (pair_ref, pair)]
    for n in range(4):
        part = pl.ds(n * step, step)
        moves.append((gathered_ref.at[part], gathered.at[part]))
    copies = [pltpu.make_async_copy(a, b, sems.at[n]) for n, (a, b) in enumerate(moves)]
    for copy in copies:
        copy.start()
    copies[0].wait()
    copies[1].wait()
    for n in range(4):
        copies[2 + n].wait()
        block = gathered[n * step : (n + 1) * step].reshape(step * rows, width)
        for weight, lanes in ((query, slice(0, 512)), (pair, slice(512, 640))):
            part = jnp.dot(block, weight[...], preferred_element_type=F32)
            part = part.astype(BF).reshape(step, 2, half, part.shape[1])
            for core in range(2):

                @pl.when(place_ref[0] == core)
                def _():
                    keep_ref[n * step : (n + 1) * step, :, lanes] = part[:, core]
                    send_ref[n * step : (n + 1) * step, :, lanes] = part[:, 1 - core]


def project(place, *operands):
    return pl.pallas_call(
        project_kernel,
        out_shape=[jax.ShapeDtypeStruct((16, 16, 640), BF)] * 2,
        in_specs=[SMEM] + [HBM] * 3,
        out_specs=[VMEM] * 2,
        scratch_shapes=[pltpu.VMEM(x.shape, BF) for x in operands] + [pltpu.SemaphoreType.DMA((6,))],
        compiler_params=FULL,
        name="project",
    )(place, *operands)


def pick(places, place, cache):
    prompts, chunk = cache.shape[:2]

    def pick_kernel(place_ref, cache_ref, *pieces):
        for k, piece_ref in zip(places, pieces):
            for g in range(2):
                at = pl.multiple_of((place_ref[0] ^ k) * 256 + g * HEAD_DIM, HEAD_DIM)
                block = cache_ref[0, :, :, pl.ds(at, HEAD_DIM)]
                for v in range(2):
                    piece_ref[0, v, g] = block[:, v, :]

    block = pl.BlockSpec((1, 2, 2, chunk, HEAD_DIM), lambda p: (p, 0, 0, 0, 0))
    return pl.pallas_call(
        pick_kernel,
        grid=(prompts,),
        out_shape=[jax.ShapeDtypeStruct((prompts, 2, 2, chunk, HEAD_DIM), BF)] * len(places),
        in_specs=[SMEM, pl.BlockSpec((1,) + cache.shape[1:], lambda p: (p, 0, 0, 0))],
        out_specs=[block] * len(places),
        compiler_params=PARAMS,
        name="pick",
    )(place, cache)


def arrange_kernel(both_ref, parts_ref):
    for j in range(4):
        for a in range(4):
            parts_ref[a, j, :, :512] = both_ref[4 * a + j, :, :512]
        pairs = [both_ref[4 * j + i, :, 512:] for i in range(4)]
        pairs = jnp.concatenate(pairs, axis=1)
        for a in range(4):
            parts_ref[a, j, :, 512:] = pairs


def arrange(both):
    return pl.pallas_call(
        arrange_kernel,
        out_shape=jax.ShapeDtypeStruct((4, 4, both.shape[1], 1024), BF),
        in_specs=[VMEM],
        out_specs=VMEM,
        compiler_params=PARAMS,
        name="arrange",
    )(both)


def attend_kernel(lengths_ref, place_ref, parts_ref, scale_ref, *refs):
    caches, out_ref, pair_ref = refs[:4], refs[4], refs[5]
    _, prompts, blocks, samples, _ = parts_ref.shape
    _, _, heads, chunk, dim = caches[0].shape
    per_block = 512 // dim
    factor = dim**-0.5
    place = place_ref[0]
    column = lax.broadcasted_iota(jnp.int32, (1, chunk), 1)
    positions = [(place ^ k) * chunk + column for k in range(len(caches))]
    for p in range(prompts):
        length = lengths_ref[0, p]
        here = slice(p * samples, (p + 1) * samples)
        scale = scale_ref[here]

        def total(block, lanes):
            part = parts_ref[0, p, block, :, lanes].astype(F32)
            part = part + parts_ref[1, p, block, :, lanes].astype(F32)
            return (part * scale).astype(BF)

        for j in range(blocks):
            pair_ref[here, j * 512 : (j + 1) * 512] = total(j, slice(512, 1024))
        for g in range(heads):
            head = place * heads + g
            lanes = pl.ds(pl.multiple_of(512 + lax.rem(head, 4) * dim, dim), dim)
            new_key = total(head // 4, lanes).astype(F32)
            new_value = total(2 + head // 4, lanes).astype(F32)
            names = [(j, h) for j in (2 * g, 2 * g + 1) for h in range(per_block)]
            queries = [total(j, slice(0, 512)) for j in (2 * g, 2 * g + 1)]
            query = [q[:, h * dim : (h + 1) * dim] for q in queries for h in range(per_block)]
            query = jnp.concatenate(query, axis=0)
            new_key = jnp.concatenate([new_key] * len(names), axis=0)
            new_value = jnp.concatenate([new_value] * len(names), axis=0)
            own = jnp.sum(query.astype(F32) * new_key, axis=1, keepdims=True) * factor
            scores = []
            top = own
            for k in range(len(caches)):
                block = lax.dot_general(
                    query, caches[k][p, 0, g], (((1,), (1,)), ((), ())), preferred_element_type=F32
                )
                block = jnp.where(positions[k] < length, block * factor, FLOOR)
                top = jnp.maximum(top, jnp.max(block, axis=1, keepdims=True))
                scores.append(block)
            own_weight = jnp.exp(own - top)
            weight_sum = own_weight
            value = own_weight.astype(BF).astype(F32) * new_value
            for k in range(len(caches)):
                weight = jnp.exp(scores[k] - top)
                weight_sum = weight_sum + jnp.sum(weight, axis=1, keepdims=True)
                value = value + jnp.dot(
                    weight.astype(BF), caches[k][p, 1, g], preferred_element_type=F32
                )
            result = (value / weight_sum).astype(BF)
            for n, (j, h) in enumerate(names):
                at = (j * per_block + h) * dim
                out_ref[here, at : at + dim] = result[n * samples : (n + 1) * samples]


def attend(lengths, place, parts, scale, caches):
    rows = parts.shape[1] * parts.shape[3]
    return pl.pallas_call(
        attend_kernel,
        out_shape=[jax.ShapeDtypeStruct((rows, 2048), BF)] * 2,
        in_specs=[SMEM, SMEM] + [VMEM] * 6,
        out_specs=(VMEM, VMEM),
        compiler_params=PARAMS,
        name="attend",
    )(lengths, place, parts, scale, *caches)


def shards(hidden_in, norm_gain, q_weight, kv_weight, kv_cache, lengths):
    rows, width = hidden_in.shape[1:]
    row_count = 4
    row_index = lax.axis_index(ROW)
    widened = hidden_in[0].astype(F32)
    sent = (widened * norm_gain[0][None, :]).astype(BF)
    local_squares = jnp.sum(widened * widened, axis=1)
    swap = [(0, 1), (1, 0)]

    count = 16
    gathered = lax.all_to_all(jnp.broadcast_to(sent[None], (count, rows, width)), COL, 0, 0)
    caches = list(pick((0, 1, 2, 3), row_index[None], kv_cache[0]))
    for k in range(1, row_count):
        caches[k] = lax.ppermute(caches[k], ROW, [(i, i ^ k) for i in range(row_count)])
    keep, send = project(lax.axis_index("co")[None], gathered, q_weight[0], kv_weight[0])
    send, caches = lax.optimization_barrier((send, caches))
    both = (keep.astype(F32) + lax.ppermute(send, "co", swap).astype(F32)).astype(BF)
    both, local_squares = lax.optimization_barrier((both, local_squares))
    both = lax.all_to_all(both, COL, 0, 0)
    squares = lax.psum(local_squares, ROW)
    both, squares = lax.optimization_barrier((both, squares))
    parts = lax.all_to_all(arrange(both), ROW, 0, 0)
    parts = parts.reshape((2, 2) + parts.shape[1:])

    scale = lax.rsqrt(squares / (width * row_count) + EPSILON)[:, None]
    attended, new_kv = attend(lengths, row_index[None], parts, scale, caches)
    count = 8
    handed = lax.ppermute(attended[None], "z", [((i - 1) % count, i) for i in range(count)])
    return (handed, new_kv[None])


def solution(mesh):
    fine = Mesh(mesh.devices.reshape(8, 2, 2, 2, 8), ("z", "xh", "co", "xl", "y"))
    return jax.shard_map(
        shards,
        mesh=fine,
        in_specs=(
            P("z", COL, ROW),
            P("z", ROW),
            P("z", ROW, COL),
            P("z", ROW, COL),
            P("z", COL, ROW, None, None),
            P("z", COL),
        ),
        out_specs=(P("z", COL, ROW), P("z", COL, None)),
        check_vma=False,
    )
```

```python
import jax
import jax.numpy as jnp
from jax import lax
from jax.experimental import pallas as pl
from jax.experimental.pallas import tpu as pltpu
from jax.sharding import Mesh
from jax.sharding import PartitionSpec as P

HEAD_DIM = 128
EPSILON = 1e-05
FLOOR = -1e30
ROW = ("xh", "co")
COL = ("xl", "y")
BF = jnp.bfloat16
F32 = jnp.float32
VMEM = pl.BlockSpec(memory_space=pltpu.VMEM)
HBM = pl.BlockSpec(memory_space=pltpu.HBM)
SMEM = pl.BlockSpec(memory_space=pltpu.SMEM)
PARAMS = pltpu.CompilerParams(vmem_limit_bytes=32 * 1024 * 1024)
MOST = pltpu.CompilerParams(vmem_limit_bytes=59 * 1024 * 1024)
FULL = pltpu.CompilerParams(vmem_limit_bytes=56 * 1024 * 1024)


def spread_kernel(hidden_ref, gain_ref, copies_ref, squares_ref, sent, sems):
    widened = hidden_ref[...].astype(F32)
    sent[...] = (widened * gain_ref[...]).astype(BF)
    copies = [
        pltpu.make_async_copy(sent, copies_ref.at[n], sems.at[n]) for n in range(copies_ref.shape[0])
    ]
    for copy in copies:
        copy.start()
    squares_ref[...] = jnp.sum(widened * widened, axis=1, keepdims=True)
    for copy in copies:
        copy.wait()


def spread(hidden, gain, count):
    rows = hidden.shape[0]
    return pl.pallas_call(
        spread_kernel,
        out_shape=[
            jax.ShapeDtypeStruct((count,) + hidden.shape, BF),
            jax.ShapeDtypeStruct((rows, 1), F32),
        ],
        in_specs=[VMEM, VMEM],
        out_specs=[HBM, VMEM],
        scratch_shapes=[pltpu.VMEM(hidden.shape, BF), pltpu.SemaphoreType.DMA((count,))],
        compiler_params=MOST,
        name="spread",
    )(hidden, gain)


def join_kernel(keep_ref, other_ref, out_ref):
    out_ref[...] = (keep_ref[...].astype(F32) + other_ref[...].astype(F32)).astype(BF)


def join(keep, other):
    return pl.pallas_call(
        join_kernel,
        out_shape=jax.ShapeDtypeStruct(keep.shape, BF),
        in_specs=[VMEM, VMEM],
        out_specs=VMEM,
        compiler_params=PARAMS,
        name="join",
    )(keep, other)


def project_kernel(place_ref, gathered_ref, query_ref, pair_ref, keep_ref, send_ref, *scratch):
    gathered, query, pair, sems = scratch
    count, rows, width = gathered_ref.shape
    half = rows // 2
    block = 256
    moves = [(gathered_ref, gathered), (query_ref.at[:, pl.ds(0, block)], query.at[:, pl.ds(0, block)])]
    moves.append((query_ref.at[:, pl.ds(block, block)], query.at[:, pl.ds(block, block)]))
    moves.append((pair_ref, pair))
    copies = [pltpu.make_async_copy(a, b, sems.at[n]) for n, (a, b) in enumerate(moves)]
    for copy in copies:
        copy.start()
    copies[0].wait()
    flat = gathered[...].reshape(count * rows, width)
    for n in range(3):
        copies[1 + n].wait()
        weight = query[:, n * block : (n + 1) * block] if n < 2 else pair[...]
        lanes = slice(n * block, n * block + weight.shape[1])
        part = jnp.dot(flat, weight, preferred_element_type=F32)
        part = part.astype(BF).reshape(count, 2, half, part.shape[1])
        for core in range(2):

            @pl.when(place_ref[0] == core)
            def _():
                keep_ref[:, :, lanes] = part[:, core]
                send_ref[:, :, lanes] = part[:, 1 - core]


def project(place, *operands):
    return pl.pallas_call(
        project_kernel,
        out_shape=[jax.ShapeDtypeStruct((16, 16, 640), BF)] * 2,
        in_specs=[SMEM] + [HBM] * 3,
        out_specs=[VMEM] * 2,
        scratch_shapes=[pltpu.VMEM(x.shape, BF) for x in operands] + [pltpu.SemaphoreType.DMA((4,))],
        compiler_params=FULL,
        name="project",
    )(place, *operands)


def pick(places, place, cache):
    prompts, chunk = cache.shape[:2]

    def pick_kernel(place_ref, cache_ref, *pieces):
        for k, piece_ref in zip(places, pieces):
            for g in range(2):
                at = pl.multiple_of((place_ref[0] ^ k) * 256 + g * HEAD_DIM, HEAD_DIM)
                block = cache_ref[0, :, :, pl.ds(at, HEAD_DIM)]
                for v in range(2):
                    piece_ref[0, v, g] = block[:, v, :]

    block = pl.BlockSpec((1, 2, 2, chunk, HEAD_DIM), lambda p: (p, 0, 0, 0, 0))
    return pl.pallas_call(
        pick_kernel,
        grid=(prompts,),
        out_shape=[jax.ShapeDtypeStruct((prompts, 2, 2, chunk, HEAD_DIM), BF)] * len(places),
        in_specs=[SMEM, pl.BlockSpec((1,) + cache.shape[1:], lambda p: (p, 0, 0, 0))],
        out_specs=[block] * len(places),
        compiler_params=PARAMS,
        name="pick",
    )(place, cache)


def arrange_kernel(both_ref, parts_ref):
    for j in range(4):
        for a in range(4):
            parts_ref[a, j, :, :512] = both_ref[4 * a + j, :, :512]
        pairs = [both_ref[4 * j + i, :, 512:] for i in range(4)]
        pairs = jnp.concatenate(pairs, axis=1)
        for a in range(4):
            parts_ref[a, j, :, 512:] = pairs


def arrange(both):
    return pl.pallas_call(
        arrange_kernel,
        out_shape=jax.ShapeDtypeStruct((4, 4, both.shape[1], 1024), BF),
        in_specs=[VMEM],
        out_specs=VMEM,
        compiler_params=PARAMS,
        name="arrange",
    )(both)


def attend_kernel(lengths_ref, place_ref, parts_ref, scale_ref, *refs):
    caches, out_ref, pair_ref = refs[:4], refs[4], refs[5]
    _, prompts, blocks, samples, _ = parts_ref.shape
    _, _, heads, chunk, dim = caches[0].shape
    per_block = 512 // dim
    factor = dim**-0.5
    place = place_ref[0]
    column = lax.broadcasted_iota(jnp.int32, (1, chunk), 1)
    positions = [(place ^ k) * chunk + column for k in range(len(caches))]
    for p in range(prompts):
        length = lengths_ref[0, p]
        here = slice(p * samples, (p + 1) * samples)
        scale = scale_ref[here]

        def total(block, lanes):
            part = parts_ref[0, p, block, :, lanes].astype(F32)
            part = part + parts_ref[1, p, block, :, lanes].astype(F32)
            return (part * scale).astype(BF)

        for j in range(blocks):
            pair_ref[here, j * 512 : (j + 1) * 512] = total(j, slice(512, 1024))
        for g in range(heads):
            head = place * heads + g
            lanes = pl.ds(pl.multiple_of(512 + lax.rem(head, 4) * dim, dim), dim)
            new_key = total(head // 4, lanes).astype(F32)
            new_value = total(2 + head // 4, lanes).astype(F32)
            names = [(j, h) for j in (2 * g, 2 * g + 1) for h in range(per_block)]
            queries = [total(j, slice(0, 512)) for j in (2 * g, 2 * g + 1)]
            query = [q[:, h * dim : (h + 1) * dim] for q in queries for h in range(per_block)]
            query = jnp.concatenate(query, axis=0)
            new_key = jnp.concatenate([new_key] * len(names), axis=0)
            new_value = jnp.concatenate([new_value] * len(names), axis=0)
            own = jnp.sum(query.astype(F32) * new_key, axis=1, keepdims=True) * factor
            scores = []
            top = own
            for k in range(len(caches)):
                block = lax.dot_general(
                    query, caches[k][p, 0, g], (((1,), (1,)), ((), ())), preferred_element_type=F32
                )
                block = jnp.where(positions[k] < length, block * factor, FLOOR)
                top = jnp.maximum(top, jnp.max(block, axis=1, keepdims=True))
                scores.append(block)
            own_weight = jnp.exp(own - top)
            weight_sum = own_weight
            value = own_weight.astype(BF).astype(F32) * new_value
            for k in range(len(caches)):
                weight = jnp.exp(scores[k] - top)
                weight_sum = weight_sum + jnp.sum(weight, axis=1, keepdims=True)
                value = value + jnp.dot(
                    weight.astype(BF), caches[k][p, 1, g], preferred_element_type=F32
                )
            result = (value / weight_sum).astype(BF)
            for n, (j, h) in enumerate(names):
                at = (j * per_block + h) * dim
                out_ref[here, at : at + dim] = result[n * samples : (n + 1) * samples]


def attend(lengths, place, parts, scale, caches):
    rows = parts.shape[1] * parts.shape[3]
    return pl.pallas_call(
        attend_kernel,
        out_shape=[jax.ShapeDtypeStruct((rows, 2048), BF)] * 2,
        in_specs=[SMEM, SMEM] + [VMEM] * 6,
        out_specs=(VMEM, VMEM),
        compiler_params=PARAMS,
        name="attend",
    )(lengths, place, parts, scale, *caches)


def shards(hidden_in, norm_gain, q_weight, kv_weight, kv_cache, lengths):
    rows, width = hidden_in.shape[1:]
    row_count = 4
    row_index = lax.axis_index(ROW)
    swap = [(0, 1), (1, 0)]
    copies, local_squares = spread(hidden_in[0], norm_gain, 16)
    gathered = lax.all_to_all(copies, COL, 0, 0)
    caches = list(pick((0, 1, 2, 3), row_index[None], kv_cache[0]))
    for k in range(1, row_count):
        caches[k] = lax.ppermute(caches[k], ROW, [(i, i ^ k) for i in range(row_count)])
    keep, send = project(lax.axis_index("co")[None], gathered, q_weight[0], kv_weight[0])
    send, caches = lax.optimization_barrier((send, caches))
    both = join(keep, lax.ppermute(send, "co", swap))
    both, local_squares = lax.optimization_barrier((both, local_squares))
    both = lax.all_to_all(both, COL, 0, 0)
    squares = lax.psum(local_squares, ROW)
    both, squares = lax.optimization_barrier((both, squares))
    parts = lax.all_to_all(arrange(both), ROW, 0, 0)
    parts = parts.reshape((2, 2) + parts.shape[1:])

    scale = lax.rsqrt(squares / (width * row_count) + EPSILON)
    attended, new_kv = attend(lengths, row_index[None], parts, scale, caches)
    count = 8
    handed = lax.ppermute(attended[None], "z", [((i - 1) % count, i) for i in range(count)])
    return (handed, new_kv[None])


def solution(mesh):
    fine = Mesh(mesh.devices.reshape(8, 2, 2, 2, 8), ("z", "xh", "co", "xl", "y"))
    return jax.shard_map(
        shards,
        mesh=fine,
        in_specs=(
            P("z", COL, ROW),
            P("z", ROW),
            P("z", ROW, COL),
            P("z", ROW, COL),
            P("z", COL, ROW, None, None),
            P("z", COL),
        ),
        out_specs=(P("z", COL, ROW), P("z", COL, None)),
        check_vma=False,
    )
```

```python
import jax
import jax.numpy as jnp
from jax import lax
from jax.experimental import pallas as pl
from jax.experimental.pallas import tpu as pltpu
from jax.sharding import Mesh
from jax.sharding import PartitionSpec as P

HEAD_DIM = 128
EPSILON = 1e-05
FLOOR = -1e30
ROW = ("xh", "co")
COL = ("xl", "y")
BF = jnp.bfloat16
F32 = jnp.float32
VMEM = pl.BlockSpec(memory_space=pltpu.VMEM)
SMEM = pl.BlockSpec(memory_space=pltpu.SMEM)
PARAMS = pltpu.CompilerParams(vmem_limit_bytes=32 * 1024 * 1024)


def project_kernel(place_ref, gathered_ref, query_ref, pair_ref, keep_ref, send_ref):
    count, rows, width = gathered_ref.shape
    half = rows // 2
    step = count // 2
    for n in range(2):
        cols = slice(n * step, (n + 1) * step)
        block = gathered_ref[cols].reshape(step * rows, width)
        for weight_ref, lanes in ((query_ref, slice(0, 512)), (pair_ref, slice(512, 640))):
            part = jnp.dot(block, weight_ref[...], preferred_element_type=F32)
            part = part.astype(BF).reshape(step, 2, half, part.shape[1])
            for core in range(2):

                @pl.when(place_ref[0] == core)
                def _():
                    keep_ref[cols, :, lanes] = part[:, core]
                    send_ref[cols, :, lanes] = part[:, 1 - core]


def project(place, *operands):
    return pl.pallas_call(
        project_kernel,
        out_shape=[jax.ShapeDtypeStruct((16, 16, 640), BF)] * 2,
        in_specs=[SMEM] + [VMEM] * 3,
        out_specs=[VMEM] * 2,
        compiler_params=PARAMS,
        name="project",
    )(place, *operands)


def pick(places, place, cache):
    prompts, chunk = cache.shape[:2]

    def pick_kernel(place_ref, cache_ref, *pieces):
        for k, piece_ref in zip(places, pieces):
            for g in range(2):
                at = pl.multiple_of((place_ref[0] ^ k) * 256 + g * HEAD_DIM, HEAD_DIM)
                block = cache_ref[0, :, :, pl.ds(at, HEAD_DIM)]
                for v in range(2):
                    piece_ref[0, v, g] = block[:, v, :]

    block = pl.BlockSpec((1, 2, 2, chunk, HEAD_DIM), lambda p: (p, 0, 0, 0, 0))
    return pl.pallas_call(
        pick_kernel,
        grid=(prompts,),
        out_shape=[jax.ShapeDtypeStruct((prompts, 2, 2, chunk, HEAD_DIM), BF)] * len(places),
        in_specs=[SMEM, pl.BlockSpec((1,) + cache.shape[1:], lambda p: (p, 0, 0, 0))],
        out_specs=[block] * len(places),
        compiler_params=PARAMS,
        name="pick",
    )(place, cache)


def arrange_kernel(both_ref, parts_ref):
    for j in range(4):
        for a in range(4):
            parts_ref[a, j, :, :512] = both_ref[4 * a + j, :, :512]
        pairs = [both_ref[4 * j + i, :, 512:] for i in range(4)]
        pairs = jnp.concatenate(pairs, axis=1)
        for a in range(4):
            parts_ref[a, j, :, 512:] = pairs


def arrange(both):
    return pl.pallas_call(
        arrange_kernel,
        out_shape=jax.ShapeDtypeStruct((4, 4, both.shape[1], 1024), BF),
        in_specs=[VMEM],
        out_specs=VMEM,
        compiler_params=PARAMS,
        name="arrange",
    )(both)


def attend_kernel(lengths_ref, place_ref, parts_ref, scale_ref, *refs):
    caches, out_ref, pair_ref = refs[:4], refs[4], refs[5]
    _, prompts, blocks, samples, _ = parts_ref.shape
    _, _, heads, chunk, dim = caches[0].shape
    per_block = 512 // dim
    factor = dim**-0.5
    place = place_ref[0]
    column = lax.broadcasted_iota(jnp.int32, (1, chunk), 1)
    positions = [(place ^ k) * chunk + column for k in range(len(caches))]
    for p in range(prompts):
        length = lengths_ref[0, p]
        here = slice(p * samples, (p + 1) * samples)
        scale = scale_ref[here]

        def total(block, lanes):
            part = parts_ref[0, p, block, :, lanes].astype(F32)
            part = part + parts_ref[1, p, block, :, lanes].astype(F32)
            return (part * scale).astype(BF)

        for j in range(blocks):
            pair_ref[here, j * 512 : (j + 1) * 512] = total(j, slice(512, 1024))
        for g in range(heads):
            head = place * heads + g
            lanes = pl.ds(pl.multiple_of(512 + lax.rem(head, 4) * dim, dim), dim)
            new_key = total(head // 4, lanes).astype(F32)
            new_value = total(2 + head // 4, lanes).astype(F32)
            names = [(j, h) for j in (2 * g, 2 * g + 1) for h in range(per_block)]
            queries = [total(j, slice(0, 512)) for j in (2 * g, 2 * g + 1)]
            query = [q[:, h * dim : (h + 1) * dim] for q in queries for h in range(per_block)]
            query = jnp.concatenate(query, axis=0)
            new_key = jnp.concatenate([new_key] * len(names), axis=0)
            new_value = jnp.concatenate([new_value] * len(names), axis=0)
            own = jnp.sum(query.astype(F32) * new_key, axis=1, keepdims=True) * factor
            scores = []
            top = own
            for k in range(len(caches)):
                block = lax.dot_general(
                    query, caches[k][p, 0, g], (((1,), (1,)), ((), ())), preferred_element_type=F32
                )
                block = jnp.where(positions[k] < length, block * factor, FLOOR)
                top = jnp.maximum(top, jnp.max(block, axis=1, keepdims=True))
                scores.append(block)
            own_weight = jnp.exp(own - top)
            weight_sum = own_weight
            value = own_weight.astype(BF).astype(F32) * new_value
            for k in range(len(caches)):
                weight = jnp.exp(scores[k] - top)
                weight_sum = weight_sum + jnp.sum(weight, axis=1, keepdims=True)
                value = value + jnp.dot(
                    weight.astype(BF), caches[k][p, 1, g], preferred_element_type=F32
                )
            result = (value / weight_sum).astype(BF)
            for n, (j, h) in enumerate(names):
                at = (j * per_block + h) * dim
                out_ref[here, at : at + dim] = result[n * samples : (n + 1) * samples]


def attend(lengths, place, parts, scale, caches):
    rows = parts.shape[1] * parts.shape[3]
    return pl.pallas_call(
        attend_kernel,
        out_shape=[jax.ShapeDtypeStruct((rows, 2048), BF)] * 2,
        in_specs=[SMEM, SMEM] + [VMEM] * 6,
        out_specs=(VMEM, VMEM),
        compiler_params=PARAMS,
        name="attend",
    )(lengths, place, parts, scale, *caches)


def shards(hidden_in, norm_gain, q_weight, kv_weight, kv_cache, lengths):
    rows, width = hidden_in.shape[1:]
    row_count = 4
    row_index = lax.axis_index(ROW)
    widened = hidden_in[0].astype(F32)
    sent = (widened * norm_gain[0][None, :]).astype(BF)
    local_squares = jnp.sum(widened * widened, axis=1)
    swap = [(0, 1), (1, 0)]

    count = 16
    gathered = lax.all_to_all(jnp.broadcast_to(sent[None], (count, rows, width)), COL, 0, 0)
    caches = list(pick((0, 1, 2, 3), row_index[None], kv_cache[0]))
    for k in range(1, row_count):
        caches[k] = lax.ppermute(caches[k], ROW, [(i, i ^ k) for i in range(row_count)])
    keep, send = project(lax.axis_index("co")[None], gathered, q_weight[0], kv_weight[0])
    send, caches = lax.optimization_barrier((send, caches))
    both = (keep.astype(F32) + lax.ppermute(send, "co", swap).astype(F32)).astype(BF)
    both, local_squares = lax.optimization_barrier((both, local_squares))
    both = lax.all_to_all(both, COL, 0, 0)
    squares = lax.psum(local_squares, ROW)
    both, squares = lax.optimization_barrier((both, squares))
    parts = lax.all_to_all(arrange(both), ROW, 0, 0)
    parts = parts.reshape((2, 2) + parts.shape[1:])

    scale = lax.rsqrt(squares / (width * row_count) + EPSILON)[:, None]
    attended, new_kv = attend(lengths, row_index[None], parts, scale, caches)
    count = 8
    handed = lax.ppermute(attended[None], "z", [((i - 1) % count, i) for i in range(count)])
    return (handed, new_kv[None])


def solution(mesh):
    fine = Mesh(mesh.devices.reshape(8, 2, 2, 2, 8), ("z", "xh", "co", "xl", "y"))
    return jax.shard_map(
        shards,
        mesh=fine,
        in_specs=(
            P("z", COL, ROW),
            P("z", ROW),
            P("z", ROW, COL),
            P("z", ROW, COL),
            P("z", COL, ROW, None, None),
            P("z", COL),
        ),
        out_specs=(P("z", COL, ROW), P("z", COL, None)),
        check_vma=False,
    )
```

```python
import jax
import jax.numpy as jnp
from jax import lax
from jax.experimental import pallas as pl
from jax.experimental.pallas import tpu as pltpu
from jax.sharding import Mesh
from jax.sharding import PartitionSpec as P

HEAD_DIM = 128
EPSILON = 1e-05
FLOOR = -1e30
ROW = ("xh", "co")
COL = ("xl", "y")
BF = jnp.bfloat16
F32 = jnp.float32
VMEM = pl.BlockSpec(memory_space=pltpu.VMEM)
SMEM = pl.BlockSpec(memory_space=pltpu.SMEM)
MOST = pltpu.CompilerParams(vmem_limit_bytes=59 * 1024 * 1024)
PARAMS = pltpu.CompilerParams(vmem_limit_bytes=32 * 1024 * 1024)


def project_kernel(place_ref, gathered_ref, query_ref, pair_ref, keep_ref, send_ref):
    count, rows, width = gathered_ref.shape
    half = rows // 2
    step = count // 2
    for n in range(2):
        cols = slice(n * step, (n + 1) * step)
        block = gathered_ref[cols].reshape(step * rows, width)
        for weight_ref, lanes in ((query_ref, slice(0, 512)), (pair_ref, slice(512, 640))):
            part = jnp.dot(block, weight_ref[...], preferred_element_type=F32)
            part = part.astype(BF).reshape(step, 2, half, part.shape[1])
            for core in range(2):

                @pl.when(place_ref[0] == core)
                def _():
                    keep_ref[cols, :, lanes] = part[:, core]
                    send_ref[cols, :, lanes] = part[:, 1 - core]


def project(place, *operands):
    return pl.pallas_call(
        project_kernel,
        out_shape=[jax.ShapeDtypeStruct((16, 16, 640), BF)] * 2,
        in_specs=[SMEM] + [VMEM] * 3,
        out_specs=[VMEM] * 2,
        compiler_params=PARAMS,
        name="project",
    )(place, *operands)


def pick(places, place, cache):
    prompts, chunk = cache.shape[:2]

    def pick_kernel(place_ref, cache_ref, *pieces):
        for k, piece_ref in zip(places, pieces):
            for g in range(2):
                at = pl.multiple_of((place_ref[0] ^ k) * 256 + g * HEAD_DIM, HEAD_DIM)
                block = cache_ref[0, :, :, pl.ds(at, HEAD_DIM)]
                for v in range(2):
                    piece_ref[0, v, g] = block[:, v, :]

    block = pl.BlockSpec((1, 2, 2, chunk, HEAD_DIM), lambda p: (p, 0, 0, 0, 0))
    return pl.pallas_call(
        pick_kernel,
        grid=(prompts,),
        out_shape=[jax.ShapeDtypeStruct((prompts, 2, 2, chunk, HEAD_DIM), BF)] * len(places),
        in_specs=[SMEM, pl.BlockSpec((1,) + cache.shape[1:], lambda p: (p, 0, 0, 0))],
        out_specs=[block] * len(places),
        compiler_params=MOST,
        name="pick",
    )(place, cache)


def arrange_kernel(both_ref, parts_ref):
    for j in range(4):
        for a in range(4):
            parts_ref[a, j, :, :512] = both_ref[4 * a + j, :, :512]
        pairs = [both_ref[4 * j + i, :, 512:] for i in range(4)]
        pairs = jnp.concatenate(pairs, axis=1)
        for a in range(4):
            parts_ref[a, j, :, 512:] = pairs


def arrange(both):
    return pl.pallas_call(
        arrange_kernel,
        out_shape=jax.ShapeDtypeStruct((4, 4, both.shape[1], 1024), BF),
        in_specs=[VMEM],
        out_specs=VMEM,
        compiler_params=PARAMS,
        name="arrange",
    )(both)


def attend_kernel(lengths_ref, place_ref, parts_ref, scale_ref, *refs):
    caches, out_ref, pair_ref = refs[:4], refs[4], refs[5]
    _, prompts, blocks, samples, _ = parts_ref.shape
    _, _, heads, chunk, dim = caches[0].shape
    per_block = 512 // dim
    factor = dim**-0.5
    place = place_ref[0]
    column = lax.broadcasted_iota(jnp.int32, (1, chunk), 1)
    positions = [(place ^ k) * chunk + column for k in range(len(caches))]
    for p in range(prompts):
        length = lengths_ref[0, p]
        here = slice(p * samples, (p + 1) * samples)
        scale = scale_ref[here]

        def total(block, lanes):
            part = parts_ref[0, p, block, :, lanes].astype(F32)
            part = part + parts_ref[1, p, block, :, lanes].astype(F32)
            return (part * scale).astype(BF)

        for j in range(blocks):
            pair_ref[here, j * 512 : (j + 1) * 512] = total(j, slice(512, 1024))
        for g in range(heads):
            head = place * heads + g
            lanes = pl.ds(pl.multiple_of(512 + lax.rem(head, 4) * dim, dim), dim)
            new_key = total(head // 4, lanes).astype(F32)
            new_value = total(2 + head // 4, lanes).astype(F32)
            names = [(j, h) for j in (2 * g, 2 * g + 1) for h in range(per_block)]
            queries = [total(j, slice(0, 512)) for j in (2 * g, 2 * g + 1)]
            query = [q[:, h * dim : (h + 1) * dim] for q in queries for h in range(per_block)]
            query = jnp.concatenate(query, axis=0)
            new_key = jnp.concatenate([new_key] * len(names), axis=0)
            new_value = jnp.concatenate([new_value] * len(names), axis=0)
            own = jnp.sum(query.astype(F32) * new_key, axis=1, keepdims=True) * factor
            scores = []
            top = own
            for k in range(len(caches)):
                block = lax.dot_general(
                    query, caches[k][p, 0, g], (((1,), (1,)), ((), ())), preferred_element_type=F32
                )
                block = jnp.where(positions[k] < length, block * factor, FLOOR)
                top = jnp.maximum(top, jnp.max(block, axis=1, keepdims=True))
                scores.append(block)
            own_weight = jnp.exp(own - top)
            weight_sum = own_weight
            value = own_weight.astype(BF).astype(F32) * new_value
            for k in range(len(caches)):
                weight = jnp.exp(scores[k] - top)
                weight_sum = weight_sum + jnp.sum(weight, axis=1, keepdims=True)
                value = value + jnp.dot(
                    weight.astype(BF), caches[k][p, 1, g], preferred_element_type=F32
                )
            result = (value / weight_sum).astype(BF)
            for n, (j, h) in enumerate(names):
                at = (j * per_block + h) * dim
                out_ref[here, at : at + dim] = result[n * samples : (n + 1) * samples]


def attend(lengths, place, parts, scale, caches):
    rows = parts.shape[1] * parts.shape[3]
    return pl.pallas_call(
        attend_kernel,
        out_shape=[jax.ShapeDtypeStruct((rows, 2048), BF)] * 2,
        in_specs=[SMEM, SMEM] + [VMEM] * 6,
        out_specs=(VMEM, VMEM),
        compiler_params=PARAMS,
        name="attend",
    )(lengths, place, parts, scale, *caches)


def shards(hidden_in, norm_gain, q_weight, kv_weight, kv_cache, lengths):
    rows, width = hidden_in.shape[1:]
    row_count = 4
    row_index = lax.axis_index(ROW)
    widened = hidden_in[0].astype(F32)
    sent = (widened * norm_gain[0][None, :]).astype(BF)
    local_squares = jnp.sum(widened * widened, axis=1)
    swap = [(0, 1), (1, 0)]

    count = 16
    gathered = lax.all_to_all(jnp.broadcast_to(sent[None], (count, rows, width)), COL, 0, 0)
    caches = list(pick((0, 1, 2, 3), row_index[None], kv_cache[0]))
    for k in (2, 3, 1):
        caches[k] = lax.ppermute(caches[k], ROW, [(i, i ^ k) for i in range(row_count)])
    keep, send = project(lax.axis_index("co")[None], gathered, q_weight[0], kv_weight[0])
    send, *moved = lax.optimization_barrier((send, caches[0], caches[2], caches[3], caches[1]))
    caches = [moved[0], moved[3], moved[1], moved[2]]
    both = (keep.astype(F32) + lax.ppermute(send, "co", swap).astype(F32)).astype(BF)
    both, local_squares = lax.optimization_barrier((both, local_squares))
    both = lax.all_to_all(both, COL, 0, 0)
    squares = lax.psum(local_squares, ROW)
    both, squares = lax.optimization_barrier((both, squares))
    parts = lax.all_to_all(arrange(both), ROW, 0, 0)
    parts = parts.reshape((2, 2) + parts.shape[1:])

    scale = lax.rsqrt(squares / (width * row_count) + EPSILON)[:, None]
    attended, new_kv = attend(lengths, row_index[None], parts, scale, caches)
    count = 8
    handed = lax.ppermute(attended[None], "z", [((i - 1) % count, i) for i in range(count)])
    return (handed, new_kv[None])


def solution(mesh):
    fine = Mesh(mesh.devices.reshape(8, 2, 2, 2, 8), ("z", "xh", "co", "xl", "y"))
    return jax.shard_map(
        shards,
        mesh=fine,
        in_specs=(
            P("z", COL, ROW),
            P("z", ROW),
            P("z", ROW, COL),
            P("z", ROW, COL),
            P("z", COL, ROW, None, None),
            P("z", COL),
        ),
        out_specs=(P("z", COL, ROW), P("z", COL, None)),
        check_vma=False,
    )
```

```python
import jax
import jax.numpy as jnp
from jax import lax
from jax.experimental import pallas as pl
from jax.experimental.pallas import tpu as pltpu
from jax.sharding import Mesh
from jax.sharding import PartitionSpec as P

HEAD_DIM = 128
EPSILON = 1e-05
FLOOR = -1e30
ROW = ("xh", "co")
COL = ("xl", "y")
BF = jnp.bfloat16
F32 = jnp.float32
VMEM = pl.BlockSpec(memory_space=pltpu.VMEM)
SMEM = pl.BlockSpec(memory_space=pltpu.SMEM)
MOST = pltpu.CompilerParams(vmem_limit_bytes=59 * 1024 * 1024)
PARAMS = pltpu.CompilerParams(vmem_limit_bytes=32 * 1024 * 1024)


def project_kernel(place_ref, gathered_ref, query_ref, pair_ref, keep_ref, send_ref):
    count, rows, width = gathered_ref.shape
    half = rows // 2
    step = count // 2
    for n in range(2):
        cols = slice(n * step, (n + 1) * step)
        block = gathered_ref[cols].reshape(step * rows, width)
        for weight_ref, lanes in ((query_ref, slice(0, 512)), (pair_ref, slice(512, 640))):
            part = jnp.dot(block, weight_ref[...], preferred_element_type=F32)
            part = part.astype(BF).reshape(step, 2, half, part.shape[1])
            for core in range(2):

                @pl.when(place_ref[0] == core)
                def _():
                    keep_ref[cols, :, lanes] = part[:, core]
                    send_ref[cols, :, lanes] = part[:, 1 - core]


def project(place, *operands):
    return pl.pallas_call(
        project_kernel,
        out_shape=[jax.ShapeDtypeStruct((16, 16, 640), BF)] * 2,
        in_specs=[SMEM] + [VMEM] * 3,
        out_specs=[VMEM] * 2,
        compiler_params=PARAMS,
        name="project",
    )(place, *operands)


def pick(places, place, cache):
    prompts, chunk = cache.shape[:2]

    def pick_kernel(place_ref, cache_ref, *pieces):
        for k, piece_ref in zip(places, pieces):
            for g in range(2):
                at = pl.multiple_of((place_ref[0] ^ k) * 256 + g * HEAD_DIM, HEAD_DIM)
                block = cache_ref[0, :, :, pl.ds(at, HEAD_DIM)]
                for v in range(2):
                    piece_ref[0, v, g] = block[:, v, :]

    step = 64
    block = pl.BlockSpec((1, 2, 2, step, HEAD_DIM), lambda p, i: (p, 0, 0, i, 0))
    return pl.pallas_call(
        pick_kernel,
        grid=(prompts, chunk // step),
        out_shape=[jax.ShapeDtypeStruct((prompts, 2, 2, chunk, HEAD_DIM), BF)] * len(places),
        in_specs=[SMEM, pl.BlockSpec((1, step) + cache.shape[2:], lambda p, i: (p, i, 0, 0))],
        out_specs=[block] * len(places),
        compiler_params=MOST,
        name="pick",
    )(place, cache)


def arrange_kernel(both_ref, parts_ref):
    for j in range(4):
        for a in range(4):
            parts_ref[a, j, :, :512] = both_ref[4 * a + j, :, :512]
        pairs = [both_ref[4 * j + i, :, 512:] for i in range(4)]
        pairs = jnp.concatenate(pairs, axis=1)
        for a in range(4):
            parts_ref[a, j, :, 512:] = pairs


def arrange(both):
    return pl.pallas_call(
        arrange_kernel,
        out_shape=jax.ShapeDtypeStruct((4, 4, both.shape[1], 1024), BF),
        in_specs=[VMEM],
        out_specs=VMEM,
        compiler_params=PARAMS,
        name="arrange",
    )(both)


def attend_kernel(lengths_ref, place_ref, parts_ref, scale_ref, *refs):
    caches, out_ref, pair_ref = refs[:4], refs[4], refs[5]
    _, prompts, blocks, samples, _ = parts_ref.shape
    _, _, heads, chunk, dim = caches[0].shape
    per_block = 512 // dim
    factor = dim**-0.5
    place = place_ref[0]
    column = lax.broadcasted_iota(jnp.int32, (1, chunk), 1)
    positions = [(place ^ k) * chunk + column for k in range(len(caches))]
    for p in range(prompts):
        length = lengths_ref[0, p]
        here = slice(p * samples, (p + 1) * samples)
        scale = scale_ref[here]

        def total(block, lanes):
            part = parts_ref[0, p, block, :, lanes].astype(F32)
            part = part + parts_ref[1, p, block, :, lanes].astype(F32)
            return (part * scale).astype(BF)

        for j in range(blocks):
            pair_ref[here, j * 512 : (j + 1) * 512] = total(j, slice(512, 1024))
        for g in range(heads):
            head = place * heads + g
            lanes = pl.ds(pl.multiple_of(512 + lax.rem(head, 4) * dim, dim), dim)
            new_key = total(head // 4, lanes).astype(F32)
            new_value = total(2 + head // 4, lanes).astype(F32)
            names = [(j, h) for j in (2 * g, 2 * g + 1) for h in range(per_block)]
            queries = [total(j, slice(0, 512)) for j in (2 * g, 2 * g + 1)]
            query = [q[:, h * dim : (h + 1) * dim] for q in queries for h in range(per_block)]
            query = jnp.concatenate(query, axis=0)
            new_key = jnp.concatenate([new_key] * len(names), axis=0)
            new_value = jnp.concatenate([new_value] * len(names), axis=0)
            own = jnp.sum(query.astype(F32) * new_key, axis=1, keepdims=True) * factor
            scores = []
            top = own
            for k in range(len(caches)):
                block = lax.dot_general(
                    query, caches[k][p, 0, g], (((1,), (1,)), ((), ())), preferred_element_type=F32
                )
                block = jnp.where(positions[k] < length, block * factor, FLOOR)
                top = jnp.maximum(top, jnp.max(block, axis=1, keepdims=True))
                scores.append(block)
            own_weight = jnp.exp(own - top)
            weight_sum = own_weight
            value = own_weight.astype(BF).astype(F32) * new_value
            for k in range(len(caches)):
                weight = jnp.exp(scores[k] - top)
                weight_sum = weight_sum + jnp.sum(weight, axis=1, keepdims=True)
                value = value + jnp.dot(
                    weight.astype(BF), caches[k][p, 1, g], preferred_element_type=F32
                )
            result = (value / weight_sum).astype(BF)
            for n, (j, h) in enumerate(names):
                at = (j * per_block + h) * dim
                out_ref[here, at : at + dim] = result[n * samples : (n + 1) * samples]


def attend(lengths, place, parts, scale, caches):
    rows = parts.shape[1] * parts.shape[3]
    return pl.pallas_call(
        attend_kernel,
        out_shape=[jax.ShapeDtypeStruct((rows, 2048), BF)] * 2,
        in_specs=[SMEM, SMEM] + [VMEM] * 6,
        out_specs=(VMEM, VMEM),
        compiler_params=PARAMS,
        name="attend",
    )(lengths, place, parts, scale, *caches)


def shards(hidden_in, norm_gain, q_weight, kv_weight, kv_cache, lengths):
    rows, width = hidden_in.shape[1:]
    row_count = 4
    row_index = lax.axis_index(ROW)
    widened = hidden_in[0].astype(F32)
    sent = (widened * norm_gain[0][None, :]).astype(BF)
    local_squares = jnp.sum(widened * widened, axis=1)
    swap = [(0, 1), (1, 0)]

    count = 16
    gathered = lax.all_to_all(jnp.broadcast_to(sent[None], (count, rows, width)), COL, 0, 0)
    caches = list(pick((0, 1, 2, 3), row_index[None], kv_cache[0]))
    for k in (2, 3, 1):
        caches[k] = lax.ppermute(caches[k], ROW, [(i, i ^ k) for i in range(row_count)])
    keep, send = project(lax.axis_index("co")[None], gathered, q_weight[0], kv_weight[0])
    send, *moved = lax.optimization_barrier((send, caches[0], caches[2], caches[3], caches[1]))
    caches = [moved[0], moved[3], moved[1], moved[2]]
    both = (keep.astype(F32) + lax.ppermute(send, "co", swap).astype(F32)).astype(BF)
    both, local_squares = lax.optimization_barrier((both, local_squares))
    both = lax.all_to_all(both, COL, 0, 0)
    squares = lax.psum(local_squares, ROW)
    both, squares = lax.optimization_barrier((both, squares))
    parts = lax.all_to_all(arrange(both), ROW, 0, 0)
    parts = parts.reshape((2, 2) + parts.shape[1:])

    scale = lax.rsqrt(squares / (width * row_count) + EPSILON)[:, None]
    attended, new_kv = attend(lengths, row_index[None], parts, scale, caches)
    count = 8
    handed = lax.ppermute(attended[None], "z", [((i - 1) % count, i) for i in range(count)])
    return (handed, new_kv[None])


def solution(mesh):
    fine = Mesh(mesh.devices.reshape(8, 2, 2, 2, 8), ("z", "xh", "co", "xl", "y"))
    return jax.shard_map(
        shards,
        mesh=fine,
        in_specs=(
            P("z", COL, ROW),
            P("z", ROW),
            P("z", ROW, COL),
            P("z", ROW, COL),
            P("z", COL, ROW, None, None),
            P("z", COL),
        ),
        out_specs=(P("z", COL, ROW), P("z", COL, None)),
        check_vma=False,
    )
```

```python
import jax
import jax.numpy as jnp
from jax import lax
from jax.experimental import pallas as pl
from jax.experimental.pallas import tpu as pltpu
from jax.sharding import Mesh
from jax.sharding import PartitionSpec as P

HEAD_DIM = 128
EPSILON = 1e-05
FLOOR = -1e30
ROW = ("xh", "co")
COL = ("xl", "y")
BF = jnp.bfloat16
F32 = jnp.float32
VMEM = pl.BlockSpec(memory_space=pltpu.VMEM)
SMEM = pl.BlockSpec(memory_space=pltpu.SMEM)
MOST = pltpu.CompilerParams(vmem_limit_bytes=59 * 1024 * 1024)
PARAMS = pltpu.CompilerParams(vmem_limit_bytes=32 * 1024 * 1024)


def project_kernel(place_ref, gathered_ref, query_ref, pair_ref, keep_ref, send_ref):
    count, rows, width = gathered_ref.shape
    half = rows // 2
    step = count // 2
    for n in range(2):
        cols = slice(n * step, (n + 1) * step)
        block = gathered_ref[cols].reshape(step * rows, width)
        for weight_ref, lanes in ((query_ref, slice(0, 512)), (pair_ref, slice(512, 640))):
            part = jnp.dot(block, weight_ref[...], preferred_element_type=F32)
            part = part.astype(BF).reshape(step, 2, half, part.shape[1])
            for core in range(2):

                @pl.when(place_ref[0] == core)
                def _():
                    keep_ref[cols, :, lanes] = part[:, core]
                    send_ref[cols, :, lanes] = part[:, 1 - core]


def project(place, *operands):
    return pl.pallas_call(
        project_kernel,
        out_shape=[jax.ShapeDtypeStruct((16, 16, 640), BF)] * 2,
        in_specs=[SMEM] + [VMEM] * 3,
        out_specs=[VMEM] * 2,
        compiler_params=PARAMS,
        name="project",
    )(place, *operands)


def pick(places, place, cache):
    prompts, chunk = cache.shape[:2]

    def pick_kernel(place_ref, cache_ref, *pieces):
        for k, piece_ref in zip(places, pieces):
            for g in range(2):
                at = pl.multiple_of((place_ref[0] ^ k) * 256 + g * HEAD_DIM, HEAD_DIM)
                block = cache_ref[0, :, :, pl.ds(at, HEAD_DIM)]
                for v in range(2):
                    piece_ref[0, v, g] = block[:, v, :]

    block = pl.BlockSpec((1, 2, 2, chunk, HEAD_DIM), lambda p: (p, 0, 0, 0, 0))
    return pl.pallas_call(
        pick_kernel,
        grid=(prompts,),
        out_shape=[jax.ShapeDtypeStruct((prompts, 2, 2, chunk, HEAD_DIM), BF)] * len(places),
        in_specs=[SMEM, pl.BlockSpec((1,) + cache.shape[1:], lambda p: (p, 0, 0, 0))],
        out_specs=[block] * len(places),
        compiler_params=MOST,
        name="pick",
    )(place, cache)


def arrange_kernel(both_ref, parts_ref):
    for j in range(4):
        for a in range(4):
            parts_ref[a, j, :, :512] = both_ref[4 * a + j, :, :512]
        pairs = [both_ref[4 * j + i, :, 512:] for i in range(4)]
        pairs = jnp.concatenate(pairs, axis=1)
        for a in range(4):
            parts_ref[a, j, :, 512:] = pairs


def arrange(both):
    return pl.pallas_call(
        arrange_kernel,
        out_shape=jax.ShapeDtypeStruct((4, 4, both.shape[1], 1024), BF),
        in_specs=[VMEM],
        out_specs=VMEM,
        compiler_params=PARAMS,
        name="arrange",
    )(both)


def attend_kernel(lengths_ref, place_ref, parts_ref, scale_ref, *refs):
    sources, out_ref, pair_ref, caches, sems = refs[:4], refs[4], refs[5], refs[6:10], refs[10]
    copies = [
        pltpu.make_async_copy(source, cache, sems.at[k])
        for k, (source, cache) in enumerate(zip(sources, caches))
    ]
    for copy in copies:
        copy.start()
    _, prompts, blocks, samples, _ = parts_ref.shape
    _, _, heads, chunk, dim = caches[0].shape
    per_block = 512 // dim
    factor = dim**-0.5
    place = place_ref[0]
    column = lax.broadcasted_iota(jnp.int32, (1, chunk), 1)
    positions = [(place ^ k) * chunk + column for k in range(len(caches))]
    for p in range(prompts):
        length = lengths_ref[0, p]
        here = slice(p * samples, (p + 1) * samples)
        scale = scale_ref[here]

        def total(block, lanes):
            part = parts_ref[0, p, block, :, lanes].astype(F32)
            part = part + parts_ref[1, p, block, :, lanes].astype(F32)
            return (part * scale).astype(BF)

        for j in range(blocks):
            pair_ref[here, j * 512 : (j + 1) * 512] = total(j, slice(512, 1024))
        for g in range(heads):
            head = place * heads + g
            lanes = pl.ds(pl.multiple_of(512 + lax.rem(head, 4) * dim, dim), dim)
            new_key = total(head // 4, lanes).astype(F32)
            new_value = total(2 + head // 4, lanes).astype(F32)
            names = [(j, h) for j in (2 * g, 2 * g + 1) for h in range(per_block)]
            queries = [total(j, slice(0, 512)) for j in (2 * g, 2 * g + 1)]
            query = [q[:, h * dim : (h + 1) * dim] for q in queries for h in range(per_block)]
            query = jnp.concatenate(query, axis=0)
            new_key = jnp.concatenate([new_key] * len(names), axis=0)
            new_value = jnp.concatenate([new_value] * len(names), axis=0)
            own = jnp.sum(query.astype(F32) * new_key, axis=1, keepdims=True) * factor
            scores = []
            top = own
            for k in range(len(caches)):
                if p == 0 and g == 0:
                    copies[k].wait()
                block = lax.dot_general(
                    query, caches[k][p, 0, g], (((1,), (1,)), ((), ())), preferred_element_type=F32
                )
                block = jnp.where(positions[k] < length, block * factor, FLOOR)
                top = jnp.maximum(top, jnp.max(block, axis=1, keepdims=True))
                scores.append(block)
            own_weight = jnp.exp(own - top)
            weight_sum = own_weight
            value = own_weight.astype(BF).astype(F32) * new_value
            for k in range(len(caches)):
                weight = jnp.exp(scores[k] - top)
                weight_sum = weight_sum + jnp.sum(weight, axis=1, keepdims=True)
                value = value + jnp.dot(
                    weight.astype(BF), caches[k][p, 1, g], preferred_element_type=F32
                )
            result = (value / weight_sum).astype(BF)
            for n, (j, h) in enumerate(names):
                at = (j * per_block + h) * dim
                out_ref[here, at : at + dim] = result[n * samples : (n + 1) * samples]


def attend(lengths, place, parts, scale, caches):
    rows = parts.shape[1] * parts.shape[3]
    return pl.pallas_call(
        attend_kernel,
        out_shape=[jax.ShapeDtypeStruct((rows, 2048), BF)] * 2,
        in_specs=[SMEM, SMEM, VMEM, VMEM] + [pl.BlockSpec(memory_space=pltpu.HBM)] * 4,
        out_specs=(VMEM, VMEM),
        scratch_shapes=[pltpu.VMEM(c.shape, BF) for c in caches] + [pltpu.SemaphoreType.DMA((4,))],
        compiler_params=PARAMS,
        name="attend",
    )(lengths, place, parts, scale, *caches)


def shards(hidden_in, norm_gain, q_weight, kv_weight, kv_cache, lengths):
    rows, width = hidden_in.shape[1:]
    row_count = 4
    row_index = lax.axis_index(ROW)
    widened = hidden_in[0].astype(F32)
    sent = (widened * norm_gain[0][None, :]).astype(BF)
    local_squares = jnp.sum(widened * widened, axis=1)
    swap = [(0, 1), (1, 0)]

    count = 16
    gathered = lax.all_to_all(jnp.broadcast_to(sent[None], (count, rows, width)), COL, 0, 0)
    caches = list(pick((0, 1, 2, 3), row_index[None], kv_cache[0]))
    for k in (2, 3, 1):
        caches[k] = lax.ppermute(caches[k], ROW, [(i, i ^ k) for i in range(row_count)])
    keep, send = project(lax.axis_index("co")[None], gathered, q_weight[0], kv_weight[0])
    send, *moved = lax.optimization_barrier((send, caches[0], caches[2], caches[3], caches[1]))
    caches = [moved[0], moved[3], moved[1], moved[2]]
    both = (keep.astype(F32) + lax.ppermute(send, "co", swap).astype(F32)).astype(BF)
    both, local_squares = lax.optimization_barrier((both, local_squares))
    both = lax.all_to_all(both, COL, 0, 0)
    squares = lax.psum(local_squares, ROW)
    both, squares = lax.optimization_barrier((both, squares))
    parts = lax.all_to_all(arrange(both), ROW, 0, 0)
    parts = parts.reshape((2, 2) + parts.shape[1:])

    scale = lax.rsqrt(squares / (width * row_count) + EPSILON)[:, None]
    attended, new_kv = attend(lengths, row_index[None], parts, scale, caches)
    count = 8
    handed = lax.ppermute(attended[None], "z", [((i - 1) % count, i) for i in range(count)])
    return (handed, new_kv[None])


def solution(mesh):
    fine = Mesh(mesh.devices.reshape(8, 2, 2, 2, 8), ("z", "xh", "co", "xl", "y"))
    return jax.shard_map(
        shards,
        mesh=fine,
        in_specs=(
            P("z", COL, ROW),
            P("z", ROW),
            P("z", ROW, COL),
            P("z", ROW, COL),
            P("z", COL, ROW, None, None),
            P("z", COL),
        ),
        out_specs=(P("z", COL, ROW), P("z", COL, None)),
        check_vma=False,
    )
```
